32 devices in a mesh: fsdp: 8 (over z, x), tp: 4 (over y, core).
Axes of the slice: x: 2, y: 2, z: 4, core: 2. Of those that a mesh axis runs over, the one named last changes fastest.
Arguments:
- inputs: bfloat16 [4096, 2304], P(('fsdp', 'tp')), may hold values from -6 to 6
- segments: int32 [4096], P('fsdp'), may hold values from 0 to 5, never falling along the last dimension, each value on 1 to 2000 neighbouring positions
- cotangent: bfloat16 [4096, 2304], P(('fsdp', 'tp')), may hold values from -6 to 6
- project_weight: float32 [2304, 4, 4, 256], P('fsdp', 'tp'), may hold values from -3 to 3
- output_weight: float32 [2048, 2304], P('tp', 'fsdp'), may hold values from -0.125 to 0.125
- gate_up_weight: float32 [2304, 2, 9216], P('fsdp', None, 'tp'), may hold values from -0.125 to 0.125
- down_weight: float32 [9216, 2304], P('tp', 'fsdp'), may hold values from -0.0625 to 0.0625
- norm_gains: float32 [4, 2304], P(None, ('fsdp', 'tp')), may hold values from 0.5 to 1.5
- project_mean: float32 [2304, 4, 4, 256], P('fsdp', 'tp'), may hold values from -40 to 40
- project_power: float32 [2304, 4, 4, 256], P('fsdp', 'tp'), may hold values from 204.8 to 819.2
- output_mean: float32 [2048, 2304], P('tp', 'fsdp'), may hold values from -40 to 40
- output_power: float32 [2048, 2304], P('tp', 'fsdp'), may hold values from 204.8 to 819.2
- gate_up_mean: float32 [2304, 2, 9216], P('fsdp', None, 'tp'), may hold values from -40 to 40
- gate_up_power: float32 [2304, 2, 9216], P('fsdp', None, 'tp'), may hold values from 204.8 to 819.2
- down_mean: float32 [9216, 2304], P('tp', 'fsdp'), may hold values from -40 to 40
- down_power: float32 [9216, 2304], P('tp', 'fsdp'), may hold values from 204.8 to 819.2
- gains_mean: float32 [4, 2304], P(None, ('fsdp', 'tp')), may hold values from -40 to 40
- gains_power: float32 [4, 2304], P(None, ('fsdp', 'tp')), may hold values from 204.8 to 819.2
Outputs:
- layer_output: bfloat16 [4096, 2304], P(('fsdp', 'tp'))
- input_grad: float32 [4096, 2304], P(('fsdp', 'tp'))
- project_grad: float32 [2304, 4, 4, 256], P('fsdp', 'tp')
- project_new: float32 [2304, 4, 4, 256], P('fsdp', 'tp')
- project_mean_new: float32 [2304, 4, 4, 256], P('fsdp', 'tp')
- project_power_new: float32 [2304, 4, 4, 256], P('fsdp', 'tp')
- output_grad: float32 [2048, 2304], P('tp', 'fsdp')
- output_new: float32 [2048, 2304], P('tp', 'fsdp')
- output_mean_new: float32 [2048, 2304], P('tp', 'fsdp')
- output_power_new: float32 [2048, 2304], P('tp', 'fsdp')
- gate_up_grad: float32 [2304, 2, 9216], P('fsdp', None, 'tp')
- gate_up_new: float32 [2304, 2, 9216], P('fsdp', None, 'tp')
- gate_up_mean_new: float32 [2304, 2, 9216], P('fsdp', None, 'tp')
- gate_up_power_new: float32 [2304, 2, 9216], P('fsdp', None, 'tp')
- down_grad: float32 [9216, 2304], P('tp', 'fsdp')
- down_new: float32 [9216, 2304], P('tp', 'fsdp')
- down_mean_new: float32 [9216, 2304], P('tp', 'fsdp')
- down_power_new: float32 [9216, 2304], P('tp', 'fsdp')
- gains_grad: float32 [4, 2304], P(None, ('fsdp', 'tp'))
- gains_step: float32 [4, 2304], P(None, ('fsdp', 'tp'))
- gains_mean_new: float32 [4, 2304], P(None, ('fsdp', 'tp'))
- gains_power_new: float32 [4, 2304], P(None, ('fsdp', 'tp'))
The draws below stay inside these ranges and needn't reach their ends.
Inputs may be any that keep to these rules, and one draw needn't show every extreme that they name: `segments`: segment numbers never decrease along the tokens; one number marks one document, and a document may continue across the boundary between sequences.
All inputs are finite; a program needn't handle non-finite values.
Results may differ from the reference program's by a relative error of at most 0.025.
Values may be sent and summed in bfloat16 or wider, within the bound.
No kernel may reach another device: no remote copies, remote signals or barrier semaphores. Data moves between devices by JAX's collectives and lax.ppermute only.
A program may use at most 256 MiB of HBM per device.

```python
import math
import jax
import jax.numpy as jnp
import numpy as np
from jax import lax

D = 2304
HEADS = 8
KV = 4
HD = 256
FF = 9216
SEQ = 512
GROUP = 2
TOKENS = 4096


def draw_project_weight(key, part):
    shape = (D, KV, GROUP + 2, HD)
    base_key = jax.random.fold_in(key, 11)
    row_key = jax.random.fold_in(key, 12)
    column_key = jax.random.fold_in(key, 13)
    base = jax.random.truncated_normal(base_key, -4.0, 4.0, shape, jnp.float32) * D ** (-0.5)
    direction = jax.random.truncated_normal(row_key, -4.0, 4.0, (D, KV), jnp.float32) * D ** (-0.5)
    pattern = jax.random.truncated_normal(column_key, -3.0, 3.0, (KV, HD), jnp.float32)
    half_width = HD // 2
    places = jnp.arange(HD) % half_width
    slow_mask = (places >= half_width - HD // 8).astype(jnp.float32)
    slot_mask = (jnp.arange(GROUP + 2) <= GROUP).astype(jnp.float32)
    amplitude = 10.0 ** 0.5 * HD ** (-0.25)
    columns = pattern * slow_mask[None, :]
    extra = amplitude * direction[:, :, None, None] * columns[None, :, None, :] * slot_mask[None, None, :, None]
    return base + extra


def levels(own_key, dims, shards, low, largest):
    def one(position, parts):
        heights = jax.random.uniform(jax.random.fold_in(jax.random.fold_in(own_key, 6), position), (parts,), jnp.float32, low / len(shards), largest / len(shards))
        return jnp.repeat(jnp.exp(heights), dims[position] // parts).reshape((-1,) + (1,) * (len(dims) - position - 1))

    level = one(*shards[0])
    for cut in shards[1:]:
        level = level * one(*cut)
    return level


def profile(count, total, reach, skew):
    weights = [(1 << 20) // math.isqrt(rank ** skew) + 1 for rank in range(2, count + 1)]
    rest, counts = total - reach - (count - 1), [1] * (count - 1)
    while rest > 0:
        movable = [i for i in range(count - 1) if counts[i] < reach]
        pool, left = sum([weights[i] for i in movable]), rest
        for i in movable:
            addition = min(reach - counts[i], max(1, left * weights[i] // pool), rest)
            counts[i] = counts[i] + addition
            rest = rest - addition
    return np.array([reach] + counts)


def uneven(own_key, count, total, limit, skew):
    if count == 2:
        one = jax.random.randint(own_key, (), max(1, total - limit), min(limit, total - 1) + 1)
        return jnp.stack([one, total - one])
    lengths = jnp.asarray(profile(count, total, limit, skew), jnp.int32)
    twos = (count - 1) // 2
    donor, taker = lengths[1:1 + 2 * twos:2], lengths[2:2 + 2 * twos:2]
    margin = jnp.minimum(donor - 1, limit - taker)
    passed = jax.random.randint(jax.random.fold_in(own_key, 1), (twos,), 0, 1 << 20) % (margin + 1)
    lengths = lengths.at[1:1 + 2 * twos:2].set(donor - passed).at[2:2 + 2 * twos:2].set(taker + passed)
    return lengths[jax.random.permutation(jax.random.fold_in(own_key, 2), count)]


def centred(own_key, shape, scale, reach, shards=(), held_as=jnp.bfloat16):
    result = jax.random.normal(own_key, shape, jnp.float32) * scale
    if len(shards) > 0:
        result = levels(own_key, shape, shards, -0.22, 0.18) * result
    return jnp.clip(result, min=-reach, max=reach).astype(held_as)


def setup_inputs(seed: int = 0) -> dict:
    arg_keys = jax.random.split(jax.random.key(seed), 19)
    inputs = centred(arg_keys[0], (TOKENS, D), 1.0, 6.0, ((0, 32),))
    segments = jnp.searchsorted(jnp.cumsum(uneven(arg_keys[1], max(4, TOKENS // 600), TOKENS, min(2000, TOKENS // 2), 1)), jnp.arange(TOKENS), side="right").astype(jnp.int32)
    cotangent = centred(arg_keys[2], (TOKENS, D), 1.0, 6.0, ((0, 32),))
    project_weight = draw_project_weight(jax.random.fold_in(arg_keys[18], 71), 0)
    output_weight = centred(arg_keys[4], (HEADS * HD, D), (HEADS * HD) ** -0.5, 0.125, ((0, 4), (1, 8)), jnp.float32)
    gate_up_weight = centred(arg_keys[5], (D, 2, FF), D ** -0.5, 0.125, ((0, 8), (2, 4)), jnp.float32)
    down_weight = centred(arg_keys[6], (FF, D), FF ** -0.5, 0.0625, ((0, 4), (1, 8)), jnp.float32)
    norm_gains = jnp.clip(1.0 + 0.1 * jax.random.normal(arg_keys[7], (4, D), jnp.float32), 0.5, 1.5)
    project_mean = centred(arg_keys[8], (D, KV, GROUP + 2, HD), (0.1 * TOKENS ** 0.5), 40.0, ((0, 8), (1, 4)), jnp.float32)
    project_power = jnp.clip(jnp.exp(math.log(819.2) - 1.3862944 * jax.random.uniform(arg_keys[9], (D, KV, GROUP + 2, HD), jnp.float32) ** levels(arg_keys[9], (D, KV, GROUP + 2, HD), ((0, 8), (1, 4)), -0.2, 0.2)), 204.8, 819.2)
    output_mean = centred(arg_keys[10], (HEADS * HD, D), (0.1 * TOKENS ** 0.5), 40.0, ((0, 4), (1, 8)), jnp.float32)
    output_power = jnp.clip(jnp.exp(math.log(819.2) - 1.3862944 * jax.random.uniform(arg_keys[11], (HEADS * HD, D), jnp.float32) ** levels(arg_keys[11], (HEADS * HD, D), ((0, 4), (1, 8)), -0.2, 0.2)), 204.8, 819.2)
    gate_up_mean = centred(arg_keys[12], (D, 2, FF), (0.1 * TOKENS ** 0.5), 40.0, ((0, 8), (2, 4)), jnp.float32)
    gate_up_power = jnp.clip(jnp.exp(math.log(819.2) - 1.3862944 * jax.random.uniform(arg_keys[13], (D, 2, FF), jnp.float32) ** levels(arg_keys[13], (D, 2, FF), ((0, 8), (2, 4)), -0.2, 0.2)), 204.8, 819.2)
    down_mean = centred(arg_keys[14], (FF, D), (0.1 * TOKENS ** 0.5), 40.0, ((0, 4), (1, 8)), jnp.float32)
    down_power = jnp.clip(jnp.exp(math.log(819.2) - 1.3862944 * jax.random.uniform(arg_keys[15], (FF, D), jnp.float32) ** levels(arg_keys[15], (FF, D), ((0, 4), (1, 8)), -0.2, 0.2)), 204.8, 819.2)
    gains_mean = centred(arg_keys[16], (4, D), (0.1 * TOKENS ** 0.5), 40.0, ((1, 32),), jnp.float32)
    gains_power = jnp.clip(jnp.exp(math.log(819.2) - 1.3862944 * jax.random.uniform(arg_keys[17], (4, D), jnp.float32) ** levels(arg_keys[17], (4, D), ((1, 32),), -0.2, 0.2)), 204.8, 819.2)
    return dict(inputs=inputs, segments=segments, cotangent=cotangent, project_weight=project_weight, output_weight=output_weight, gate_up_weight=gate_up_weight, down_weight=down_weight, norm_gains=norm_gains, project_mean=project_mean, project_power=project_power, output_mean=output_mean, output_power=output_power, gate_up_mean=gate_up_mean, gate_up_power=gate_up_power, down_mean=down_mean, down_power=down_power, gains_mean=gains_mean, gains_power=gains_power)


@jax.custom_vjp
def low(v):
    return lax.optimization_barrier(v.astype(jnp.bfloat16)).astype(jnp.float32)

@jax.custom_vjp
def low_back(v):
    return v

def low_keep(v):
    return (low(v), None)

def low_pass(kept, grad):
    return (grad,)

def back_keep(v):
    return (v, None)

def back_low(kept, grad):
    return (low(grad),)
low.defvjp(low_keep, low_pass)
low_back.defvjp(back_keep, back_low)
norm_eps = 1e-06
soft_cap = 50.0
rope_base = 10000.0
beta_first = 0.9
beta_second = 0.95
learn_rate = 0.02
decay_rate = 0.1
adam_eps = 1e-08
step_number = 3.0

def rms_norm(values, gain_vec):
    factor = lax.rsqrt(lax.optimization_barrier(jnp.mean(values * values, axis=-1, keepdims=True)) + norm_eps)
    return values * factor * gain_vec

def rope_tables(length, head_width):
    half_width = head_width // 2
    frequency = rope_base ** (-2.0 * jnp.arange(half_width, dtype=jnp.float32) / head_width)
    angles = jnp.arange(length, dtype=jnp.float32)[:, None] * frequency[None, :]
    return (jnp.cos(angles), jnp.sin(angles))

def rotate(values, cosine_table, sine_table):
    half_width = values.shape[-1] // 2
    first_half = values[..., :half_width]
    second_half = values[..., half_width:]
    return jnp.concatenate([first_half * cosine_table - second_half * sine_table, second_half * cosine_table + first_half * sine_table], axis=-1)

def allowed_pairs(seg_row):
    places = jnp.arange(seg_row.shape[0])
    return (seg_row[:, None] == seg_row[None, :]) & (places[None, :] <= places[:, None])

def attend(element):
    queries, key_vectors, value_rows, seg_row = element
    highest = lax.Precision.HIGHEST
    scores = low_back(jnp.einsum('qhgd,khd->hgqk', queries, key_vectors, precision=highest))
    capped = soft_cap * jnp.tanh(scores / soft_cap)
    capped = jnp.where(allowed_pairs(seg_row), capped, -jnp.inf)
    row_max = lax.optimization_barrier(jnp.max(capped, axis=-1, keepdims=True))
    exp_scores = jnp.exp(capped - row_max)
    prob_values = low(exp_scores / lax.optimization_barrier(jnp.sum(exp_scores, axis=-1, keepdims=True)))
    return jnp.einsum('hgqk,khd->qhgd', prob_values, value_rows, precision=highest)

def layer(rows_in, seg_rows, project_low, output_low, gate_up_low, down_low, norm_gains):
    highest = lax.Precision.HIGHEST
    row_count = rows_in.shape[0]
    seq_count = row_count // SEQ
    normed_one = low(rms_norm(rows_in, norm_gains[0]))
    mixed_rows = jnp.einsum('rd,dhjc->rhjc', normed_one, project_low, precision=highest)
    shaped = mixed_rows.reshape(seq_count, SEQ, KV, GROUP + 2, HD)
    query_pre = low_back(shaped[:, :, :, :GROUP])
    key_pre = low_back(shaped[:, :, :, GROUP])
    value_rows = low(low_back(shaped[:, :, :, GROUP + 1]))
    cosine_table, sine_table = rope_tables(SEQ, HD)
    queries = low(rotate(query_pre, cosine_table[:, None, None, :], sine_table[:, None, None, :]) * HD ** (-0.5))
    key_vectors = low(rotate(key_pre, cosine_table[:, None, :], sine_table[:, None, :]))
    context = lax.map(jax.checkpoint(attend), (queries, key_vectors, value_rows, seg_rows.reshape(seq_count, SEQ)))
    context = low(low_back(context.reshape(row_count, HEADS * HD)))
    attend_sum = low_back(jnp.dot(context, output_low, precision=highest))
    hidden_state = rows_in + rms_norm(attend_sum, norm_gains[1])
    normed_two = low(rms_norm(hidden_state, norm_gains[2]))
    gate_up = jnp.einsum('rd,djf->rjf', normed_two, gate_up_low, precision=highest)
    gate_value = low_back(gate_up[:, 0])
    up_value = low_back(gate_up[:, 1])
    activated = low(jax.nn.gelu(gate_value, approximate=True) * up_value)
    feed_sum = low_back(jnp.dot(activated, down_low, precision=highest))
    return hidden_state + rms_norm(feed_sum, norm_gains[3])

def forward(rows_in, segments, project_weight, output_weight, gate_up_weight, down_weight, norm_gains):
    project_low = low(project_weight)
    output_low = low(output_weight)
    gate_up_low = low(gate_up_weight)
    down_low = low(down_weight)
    seq_total = rows_in.shape[0] // SEQ
    per_block = math.gcd(seq_total, max(1, 4096 // SEQ))
    block_count = seq_total // per_block
    blocks = rows_in.reshape(block_count, per_block * SEQ, D)
    seg_blocks = segments.reshape(block_count, per_block * SEQ)

    def one_block(element):
        return layer(element[0], element[1], project_low, output_low, gate_up_low, down_low, norm_gains)
    outcome = lax.map(jax.checkpoint(one_block), (blocks, seg_blocks))
    return outcome.reshape(rows_in.shape[0], D)

def adam_step(weight, gradient, mean_old, power_old):
    mean_new = beta_first * mean_old + (1.0 - beta_first) * gradient
    power_new = beta_second * power_old + (1.0 - beta_second) * gradient * gradient
    mean_hat = mean_new / (1.0 - beta_first ** step_number)
    power_hat = power_new / (1.0 - beta_second ** step_number)
    change = -learn_rate * (mean_hat / (jnp.sqrt(power_hat) + adam_eps) + decay_rate * weight)
    return (weight + change, mean_new, power_new, change)

def reference(inputs, segments, cotangent, project_weight, output_weight, gate_up_weight, down_weight, norm_gains, project_mean, project_power, output_mean, output_power, gate_up_mean, gate_up_power, down_mean, down_power, gains_mean, gains_power):

    def run_layer(rows_in, project_in, output_in, gate_up_in, down_in, gains_in):
        return forward(rows_in, segments, project_in, output_in, gate_up_in, down_in, gains_in)
    layer_output, pull_back = jax.vjp(run_layer, inputs.astype(jnp.float32), project_weight, output_weight, gate_up_weight, down_weight, norm_gains)
    input_grad, project_grad, output_grad, gate_up_grad, down_grad, gains_grad = pull_back(cotangent.astype(jnp.float32))
    project_new, project_mean_new, project_power_new, unused_one = adam_step(project_weight, project_grad, project_mean, project_power)
    output_new, output_mean_new, output_power_new, unused_two = adam_step(output_weight, output_grad, output_mean, output_power)
    gate_up_new, gate_up_mean_new, gate_up_power_new, unused_three = adam_step(gate_up_weight, gate_up_grad, gate_up_mean, gate_up_power)
    down_new, down_mean_new, down_power_new, unused_four = adam_step(down_weight, down_grad, down_mean, down_power)
    unused_five, gains_mean_new, gains_power_new, gains_step = adam_step(norm_gains, gains_grad, gains_mean, gains_power)
    return (layer_output.astype(jnp.bfloat16), input_grad, project_grad, project_new, project_mean_new, project_power_new, output_grad, output_new, output_mean_new, output_power_new, gate_up_grad, gate_up_new, gate_up_mean_new, gate_up_power_new, down_grad, down_new, down_mean_new, down_power_new, gains_grad, gains_step, gains_mean_new, gains_power_new)
```

```python
import jax
import jax.numpy as jnp
from jax import lax
from jax.sharding import Mesh
from jax.sharding import PartitionSpec as P

SEQ = 512

norm_eps = 1e-06
soft_cap = 50.0
rope_base = 10000.0
beta_first = 0.9
beta_second = 0.95
learn_rate = 0.02
decay_rate = 0.1
adam_eps = 1e-08
step_number = 3.0

F32 = jnp.float32
BF16 = jnp.bfloat16


def norm_forward(values, gain_vec):
    factor = lax.rsqrt(jnp.mean(values * values, axis=-1, keepdims=True) + norm_eps)
    return (values * factor * gain_vec, factor)


def norm_backward(values, factor, gain_vec, incoming):
    unit_rows = values * factor
    gain_part = jnp.sum(incoming * unit_rows, axis=0)
    scaled = incoming * gain_vec
    return (
        factor * (scaled - unit_rows * jnp.mean(scaled * unit_rows, axis=-1, keepdims=True)),
        gain_part,
    )


def rotate(values, cosine_table, sine_table):
    half_width = values.shape[-1] // 2
    first_half = values[..., :half_width]
    second_half = values[..., half_width:]
    return jnp.concatenate(
        [
            first_half * cosine_table - second_half * sine_table,
            second_half * cosine_table + first_half * sine_table,
        ],
        axis=-1,
    )


def unrotate(slopes, cosine_table, sine_table):
    return rotate(slopes, cosine_table, -sine_table)


def adam_step(weight, gradient, mean_old, power_old):
    mean_new = beta_first * mean_old + (1.0 - beta_first) * gradient
    power_new = beta_second * power_old + (1.0 - beta_second) * gradient * gradient
    mean_hat = mean_new / (1.0 - beta_first**step_number)
    power_hat = power_new / (1.0 - beta_second**step_number)
    change = -learn_rate * (mean_hat / (jnp.sqrt(power_hat) + adam_eps) + decay_rate * weight)
    return (weight + change, mean_new, power_new, change)


def swap(value, axis):
    return lax.ppermute(value, axis, [(0, 1), (1, 0)])


def from_ahead(value, axis, size, step):
    return lax.ppermute(value, axis, [(j, (j - step) % size) for j in range(size)])


def swap_two(value, first, second):
    return lax.ppermute(value, (first, second), [(0, 3), (3, 0), (1, 2), (2, 1)])


def ordered(own, other, place):
    straight = jnp.stack([own, other])
    return jnp.where(place == 0, straight, straight[::-1])


def rolled(value, place, axis):
    count = value.shape[axis]
    result = value
    for step in range(1, count):
        result = jnp.where(place == step, jnp.roll(value, -step, axis), result)
    return result


def make_device(far_size):
    def per_device(
        inputs,
        segments,
        cotangent,
        project_weight,
        output_weight,
        gate_up_weight,
        down_weight,
        norm_gains,
        project_mean,
        project_power,
        output_mean,
        output_power,
        gate_up_mean,
        gate_up_power,
        down_mean,
        down_power,
        gains_mean,
        gains_power,
    ):
        far, near, side, row, core = (lax.axis_index(name) for name in ("zh", "zl", "x", "y", "c"))
        own_rows, width = inputs.shape
        block = project_weight.shape[0]
        head_width = project_weight.shape[3]
        slots = project_weight.shape[2]
        group_size = slots - 2
        kv_local = project_weight.shape[1]
        mix_width = kv_local * slots * head_width
        context_width = output_weight.shape[0]
        hidden = down_weight.shape[0]
        half = hidden // 2
        total_rows = 4 * own_rows
        seq_count = total_rows // SEQ

        def arrange(value):
            lead = value.shape[0]
            value = value.reshape(lead, far_size, 2, 2, block).transpose(0, 3, 1, 2, 4)
            return rolled(rolled(value, side, 1), far, 2).reshape(lead, width)

        def unarrange(value):
            lead = value.shape[0]
            value = value.reshape(lead, 2, far_size, 2, block)
            value = rolled(rolled(value, side, 1), (far_size - far) % far_size, 2)
            return value.transpose(0, 2, 3, 1, 4).reshape(lead, width)

        attend_own = jnp.concatenate(
            [project_weight.astype(BF16).reshape(block, mix_width), output_weight.astype(BF16).T],
            axis=1,
        )
        rows_own = arrange(inputs)

        def gather_sequence(value):
            there = swap(value, "y")
            return jnp.concatenate([value, swap(value, "c"), there, swap(there, "c")], axis=0)

        def scatter_sequence(partial):
            part = partial.reshape(2, 2, own_rows, width)
            mine = part[:, 0] + swap(part[:, 1].astype(BF16), "c").astype(F32)
            return mine[0] + swap(mine[1].astype(BF16), "y").astype(F32)

        def gather_group(value):
            cross = [value, swap(value, "y"), swap(value, "zl"), swap_two(value, "zl", "y")]
            outer = swap(jnp.concatenate(cross[1:], axis=0), "c")
            inner = swap(value, "c")
            parts = [value, inner]
            for place in range(3):
                parts += [cross[place + 1], outer[place * own_rows : (place + 1) * own_rows]]
            return jnp.concatenate(parts, axis=0)

        def scatter_group(partial):
            part = partial.reshape(2, 2, 2, own_rows, width)
            mine = part[:, :, 0] + swap(part[:, :, 1].astype(BF16), "c").astype(F32)
            low = mine.astype(BF16)
            return (
                mine[0, 0]
                + swap(low[0, 1], "y").astype(F32)
                + swap(low[1, 0], "zl").astype(F32)
                + swap_two(low[1, 1], "zl", "y").astype(F32)
            )

        rows_in = gather_sequence(rows_own)

        gains_parts = norm_gains[None]
        for axis, place in (("c", core), ("y", row)):
            gains_parts = ordered(gains_parts, swap(gains_parts, axis), place)
        gains_parts = gains_parts.reshape((4,) + norm_gains.shape)
        gains_parts = ordered(gains_parts, swap(gains_parts, "zl"), near)
        gains_parts = jnp.stack(
            [gains_parts]
            + [from_ahead(gains_parts, "zh", far_size, step) for step in range(1, far_size)]
        )
        gains_parts = jnp.stack([gains_parts, swap(gains_parts, "x")])
        gains_all = gains_parts.reshape(-1, 4, norm_gains.shape[1]).transpose(1, 0, 2).reshape(4, width)

        attend_far = [attend_own] + [
            from_ahead(attend_own, "zh", far_size, step) for step in range(1, far_size)
        ]
        attend_side = [attend_far, [swap(piece, "x") for piece in attend_far]]
        attend_all = jnp.concatenate(
            [
                ordered(piece, swap(piece, "zl"), near).reshape(2 * block, mix_width + context_width)
                for pieces in attend_side
                for piece in pieces
            ],
            axis=0,
        )
        full_project = attend_all[:, :mix_width]
        full_output = attend_all[:, mix_width:]

        def collect(weight):
            halves = [weight[:, :half], weight[:, half:]]
            keep = jnp.where(near == 0, halves[0], halves[1])
            send = jnp.where(near == 0, halves[1], halves[0])
            own = ordered(keep, swap(send, "zl"), near).reshape(2 * block, half)
            pieces = [own] + [from_ahead(own, "zh", far_size, step) for step in range(1, far_size)]
            return jnp.concatenate(pieces + [swap(piece, "x") for piece in pieces], axis=0)

        full_gate = collect(gate_up_weight[:, 0].astype(BF16))
        full_up = collect(gate_up_weight[:, 1].astype(BF16))
        full_down = collect(down_weight.astype(BF16).T)

        residual_in = rows_own.astype(F32)
        factor_one = lax.rsqrt(jnp.mean(residual_in * residual_in, axis=-1, keepdims=True) + norm_eps)
        rows_one = norm_forward(rows_in.astype(F32), gains_all[0])[0].astype(BF16)
        mixed_rows = jnp.dot(rows_one, full_project, preferred_element_type=F32)
        query_scale = head_width ** (-0.5)
        start = jnp.stack(
            [
                ((row ^ dr) * 2 + (core ^ dc)) * own_rows
                for dr in range(2)
                for dc in range(2)
            ]
        )
        order = (start[:, None] + jnp.arange(own_rows)[None, :]).reshape(total_rows)
        seg_parts = segments.reshape(2, 2, own_rows)
        seg_parts = rolled(rolled(seg_parts, row, 0), core, 1)
        seg_rows = seg_parts.reshape(total_rows)
        places = order % SEQ
        half_width = head_width // 2
        frequency = rope_base ** (-2.0 * jnp.arange(half_width, dtype=F32) / head_width)
        angles = places.astype(F32)[:, None] * frequency[None, :]
        cosine_table, sine_table = jnp.cos(angles), jnp.sin(angles)
        shaped = mixed_rows.reshape(total_rows, kv_local, slots, head_width)
        cosine_query = cosine_table[:, None, None, :]
        sine_query = sine_table[:, None, None, :]
        cosine_key = cosine_table[:, None, :]
        sine_key = sine_table[:, None, :]
        queries = (rotate(shaped[:, :, :group_size], cosine_query, sine_query) * query_scale).astype(BF16)
        key_vectors = rotate(shaped[:, :, group_size], cosine_key, sine_key).astype(BF16)
        value_rows = shaped[:, :, group_size + 1].astype(BF16)
        allowed = (
            (seg_rows[:, None] == seg_rows[None, :])
            & (order[None, :] <= order[:, None])
            & (order[None, :] // SEQ == order[:, None] // SEQ)
        )

        scores = jnp.einsum("qhgd,khd->hgqk", queries, key_vectors, preferred_element_type=F32)
        tanh_value = jnp.tanh(scores / soft_cap)
        capped = jnp.where(allowed, soft_cap * tanh_value, -jnp.inf)
        row_max = jnp.max(capped, axis=-1, keepdims=True)
        exp_scores = jnp.exp(capped - row_max)
        row_total = jnp.sum(exp_scores, axis=-1, keepdims=True)
        prob_values = exp_scores / row_total
        context = jnp.einsum(
            "hgqk,khd->qhgd", prob_values.astype(BF16), value_rows, preferred_element_type=F32
        )
        context_flat = context.astype(BF16).reshape(total_rows, context_width)
        attend_sum = scatter_sequence(
            lax.dot_general(
                context_flat, full_output, (((1,), (1,)), ((), ())), preferred_element_type=F32
            )
        )
        post_one, factor_two = norm_forward(attend_sum, gains_all[1])
        hidden_state = residual_in + post_one
        normed_two, factor_three = norm_forward(hidden_state, gains_all[2])

        rows_two = gather_group(normed_two.astype(BF16))
        gate_value = jnp.dot(rows_two, full_gate, preferred_element_type=F32)
        up_value = jnp.dot(rows_two, full_up, preferred_element_type=F32)

        def gelu_product(gate_in, up_in):
            return jax.nn.gelu(gate_in, approximate=True) * up_in

        activated = gelu_product(gate_value, up_value).astype(BF16)
        feed_sum = scatter_group(
            lax.dot_general(activated, full_down, (((1,), (1,)), ((), ())), preferred_element_type=F32)
        )
        post_two, factor_four = norm_forward(feed_sum, gains_all[3])
        layer_output = unarrange((hidden_state + post_two).astype(BF16))

        upstream = arrange(cotangent).astype(F32)
        feed_slope, gain_four = norm_backward(feed_sum, factor_four, gains_all[3], upstream)
        feed_slope_rows = gather_group(feed_slope.astype(BF16))
        activated_slope = jnp.dot(feed_slope_rows, full_down, preferred_element_type=F32)
        unused_value, gelu_pull = jax.vjp(gelu_product, gate_value, up_value)
        gate_slope, up_slope = gelu_pull(activated_slope)
        gate_slope = gate_slope.astype(BF16)
        up_slope = up_slope.astype(BF16)
        contract_last = (((1,), (1,)), ((), ()))
        normed_two_slope = scatter_group(
            lax.dot_general(gate_slope, full_gate, contract_last, preferred_element_type=F32)
            + lax.dot_general(up_slope, full_up, contract_last, preferred_element_type=F32)
        )

        side_rows = width // 2
        far_rows = 2 * block

        def transposed(left, right):
            return lax.dot_general(left, right, (((0,), (0,)), ((), ())), preferred_element_type=F32)

        def reduce_ffn(left, right):
            sent = transposed(left[:, side_rows:], right).astype(BF16)
            kept = transposed(left[:, :side_rows], right)
            total = kept + swap(sent, "x").astype(F32)
            mine = total[:far_rows]
            low = total.astype(BF16)
            for step in range(1, far_size):
                there = low[step * far_rows : (step + 1) * far_rows]
                mine = mine + from_ahead(there, "zh", far_size, far_size - step).astype(F32)
            mine = mine.astype(BF16).reshape(2, block, half)
            keep = jnp.where(near == 0, mine[0], mine[1])
            send = jnp.where(near == 0, mine[1], mine[0])
            other = swap(send, "zl")
            first = jnp.where(near == 0, keep, other)
            second = jnp.where(near == 0, other, keep)
            return jnp.concatenate([first, second], axis=1).astype(F32)

        down_grad = reduce_ffn(feed_slope_rows, activated).T
        gate_grad = reduce_ffn(rows_two, gate_slope)
        up_grad = reduce_ffn(rows_two, up_slope)
        gate_up_grad = jnp.stack([gate_grad, up_grad], axis=1)

        hidden_part, gain_three = norm_backward(
            hidden_state, factor_three, gains_all[2], normed_two_slope
        )
        hidden_slope = upstream + hidden_part
        attend_slope, gain_two = norm_backward(attend_sum, factor_two, gains_all[1], hidden_slope)

        attend_slope_rows = gather_sequence(attend_slope.astype(BF16))
        context_slope = jnp.dot(attend_slope_rows, full_output, preferred_element_type=F32).astype(BF16)
        context_slope = context_slope.reshape(total_rows, kv_local, group_size, head_width)
        prob_slope = jnp.einsum(
            "qhgd,khd->hgqk", context_slope, value_rows, preferred_element_type=F32
        )
        value_slope = jnp.einsum(
            "hgqk,qhgd->khd", prob_values.astype(BF16), context_slope, preferred_element_type=F32
        )
        inner_sum = jnp.sum(prob_values * prob_slope, axis=-1, keepdims=True)
        score_slope = (
            prob_values * (prob_slope - inner_sum) * (1.0 - tanh_value * tanh_value)
        ).astype(BF16)
        query_slope = jnp.einsum(
            "hgqk,khd->qhgd", score_slope, key_vectors, preferred_element_type=F32
        )
        key_slope = jnp.einsum("hgqk,qhgd->khd", score_slope, queries, preferred_element_type=F32)
        query_pre_slope = unrotate(query_slope * query_scale, cosine_query, sine_query)
        key_pre_slope = unrotate(key_slope, cosine_key, sine_key)
        mixed_slope = (
            jnp.concatenate(
                [query_pre_slope, key_pre_slope[:, :, None], value_slope[:, :, None]], axis=2
            )
            .astype(BF16)
            .reshape(total_rows, mix_width)
        )
        normed_one_slope = scatter_sequence(
            lax.dot_general(mixed_slope, full_project, contract_last, preferred_element_type=F32)
        )

        def reduce_attend(left, right):
            columns = right.shape[1]
            lower = transposed(left[:, side_rows:], right).reshape(far_size, 2, block, columns)
            upper = transposed(left[:, :side_rows], right).reshape(far_size, 2, block, columns)

            def over_near(part):
                keep = jnp.where(near == 0, part[:, 0], part[:, 1])
                send = jnp.where(near == 0, part[:, 1], part[:, 0]).astype(BF16)
                return keep + swap(send, "zl").astype(F32)

            lower = over_near(lower)
            upper = over_near(upper)
            total = upper + swap(lower.astype(BF16), "x").astype(F32)
            low = total.astype(BF16)
            mine = total[0]
            for step in range(1, far_size):
                mine = mine + from_ahead(low[step], "zh", far_size, far_size - step).astype(F32)
            return mine

        output_grad = reduce_attend(attend_slope_rows, context_flat).T
        project_grad = reduce_attend(rows_one, mixed_slope).reshape(project_weight.shape)
        input_part, gain_one = norm_backward(residual_in, factor_one, gains_all[0], normed_one_slope)
        input_grad = unarrange(hidden_slope + input_part)

        gain_sum = jnp.stack([gain_one, gain_two, gain_three, gain_four], axis=0)
        gain_sum = gain_sum.reshape(4, 2, far_size, 2, 2, 2, norm_gains.shape[1])
        gain_sum = gain_sum.transpose(1, 2, 3, 4, 5, 0, 6)
        gain_sum = gain_sum[0] + swap(gain_sum[1], "x")
        gain_far = gain_sum[0]
        for step in range(1, far_size):
            gain_far = gain_far + from_ahead(gain_sum[step], "zh", far_size, far_size - step)
        for axis, place in (("zl", near), ("y", row), ("c", core)):
            keep = jnp.where(place == 0, gain_far[0], gain_far[1])
            send = jnp.where(place == 0, gain_far[1], gain_far[0])
            gain_far = keep + swap(send, axis)
        gains_grad = gain_far

        project_new, project_mean_new, project_power_new, unused_one = adam_step(
            project_weight, project_grad, project_mean, project_power
        )
        output_new, output_mean_new, output_power_new, unused_two = adam_step(
            output_weight, output_grad, output_mean, output_power
        )
        gate_up_new, gate_up_mean_new, gate_up_power_new, unused_three = adam_step(
            gate_up_weight, gate_up_grad, gate_up_mean, gate_up_power
        )
        down_new, down_mean_new, down_power_new, unused_four = adam_step(
            down_weight, down_grad, down_mean, down_power
        )
        unused_five, gains_mean_new, gains_power_new, gains_step = adam_step(
            norm_gains, gains_grad, gains_mean, gains_power
        )
        return (
            layer_output,
            input_grad,
            project_grad,
            project_new,
            project_mean_new,
            project_power_new,
            output_grad,
            output_new,
            output_mean_new,
            output_power_new,
            gate_up_grad,
            gate_up_new,
            gate_up_mean_new,
            gate_up_power_new,
            down_grad,
            down_new,
            down_mean_new,
            down_power_new,
            gains_grad,
            gains_step,
            gains_mean_new,
            gains_power_new,
        )

    return per_device


def solution(mesh):
    fsdp_size = mesh.shape["fsdp"]
    far_size = fsdp_size // 4
    fine = Mesh(mesh.devices.reshape(far_size, 2, 2, 2, 2), ("zh", "zl", "x", "y", "c"))
    fsdp = ("zh", "zl", "x")
    tp = ("y", "c")
    both = fsdp + tp
    rows = P(both, None)
    project = P(fsdp, tp, None, None)
    across = P(tp, fsdp)
    gate_up = P(fsdp, None, tp)
    gains = P(None, both)
    in_specs = (
        (rows, P(fsdp), rows, project, across, gate_up, across, gains)
        + (project,) * 2
        + (across,) * 2
        + (gate_up,) * 2
        + (across,) * 2
        + (gains,) * 2
    )
    out_specs = (
        (rows, rows)
        + (project,) * 4
        + (across,) * 4
        + (gate_up,) * 4
        + (across,) * 4
        + (gains,) * 4
    )
    return jax.shard_map(
        make_device(far_size), mesh=fine, in_specs=in_specs, out_specs=out_specs, check_vma=False
    )
```

```python
import functools

import jax
import jax.numpy as jnp
from jax import lax
from jax.experimental import pallas as pl
from jax.experimental.pallas import tpu as pltpu
from jax.sharding import Mesh
from jax.sharding import PartitionSpec as P

SEQ = 512
DEPTH = 4

norm_eps = 1e-06
soft_cap = 50.0
rope_base = 10000.0
beta_first = 0.9
beta_second = 0.95
learn_rate = 0.02
decay_rate = 0.1
adam_eps = 1e-08
step_number = 3.0

F32 = jnp.float32
BF16 = jnp.bfloat16


def norm_forward(values, gain_vec):
    factor = lax.rsqrt(jnp.mean(values * values, axis=-1, keepdims=True) + norm_eps)
    return (values * factor * gain_vec, factor)


def norm_backward(values, factor, gain_vec, incoming):
    unit_rows = values * factor
    gain_part = jnp.sum(incoming * unit_rows, axis=0)
    scaled = incoming * gain_vec
    return (
        factor * (scaled - unit_rows * jnp.mean(scaled * unit_rows, axis=-1, keepdims=True)),
        gain_part,
    )


def rotate(values, cosine_table, sine_table):
    half_width = values.shape[-1] // 2
    first_half = values[:, :half_width]
    second_half = values[:, half_width:]
    return jnp.concatenate(
        [
            first_half * cosine_table - second_half * sine_table,
            second_half * cosine_table + first_half * sine_table,
        ],
        axis=-1,
    )


def adam_step(weight, gradient, mean_old, power_old):
    mean_new = beta_first * mean_old + (1.0 - beta_first) * gradient
    power_new = beta_second * power_old + (1.0 - beta_second) * gradient * gradient
    mean_hat = mean_new / (1.0 - beta_first**step_number)
    power_hat = power_new / (1.0 - beta_second**step_number)
    change = -learn_rate * (mean_hat / (jnp.sqrt(power_hat) + adam_eps) + decay_rate * weight)
    return (weight + change, mean_new, power_new, change)


def swap(value, axis):
    return lax.ppermute(value, axis, [(0, 1), (1, 0)])


def from_ahead(value, axis, size, step):
    return lax.ppermute(value, axis, [(j, (j - step) % size) for j in range(size)])


def after(value, *others):
    return lax.optimization_barrier((value,) + others)[0]


def gated(values, *others):
    values = list(values)
    return list(lax.optimization_barrier(tuple(values) + others)[: len(values)])


def ordered(own, other, place):
    straight = jnp.stack([own, other])
    return jnp.where(place == 0, straight, straight[::-1])


def rolled(value, place, axis):
    count = value.shape[axis]
    result = value
    for step in range(1, count):
        result = jnp.where(place == step, jnp.roll(value, -step, axis), result)
    return result


def transposed(left, right):
    return lax.dot_general(left, right, (((0,), (0,)), ((), ())), preferred_element_type=F32)


def times_transposed(left, right):
    return lax.dot_general(left, right, (((1,), (1,)), ((), ())), preferred_element_type=F32)


VMEM_LIMIT = 60 * 1024 * 1024
params = pltpu.CompilerParams(vmem_limit_bytes=VMEM_LIMIT)


def whole(count):
    return [pl.BlockSpec(memory_space=pltpu.VMEM)] * count


def shape(dims, dtype=BF16):
    return jax.ShapeDtypeStruct(dims, dtype)


def dot(left, right):
    return jnp.dot(left, right, preferred_element_type=F32)


def visible(place_col, place_row, seg_col, seg_row):
    return (seg_col[...] == seg_row[...]) & (place_row[...] <= place_col[...])


def attend_kernel(
    group_size,
    head_width,
    rows,
    gain,
    weights,
    cosine,
    sine,
    place_col,
    place_row,
    seg_col,
    seg_row,
    normed_out,
    queries_out,
    keys_out,
    values_out,
    logsum_out,
    context_out,
    mine_out,
    other_out,
):
    mix_width = (group_size + 2) * head_width
    values = rows[...].astype(F32)
    normed_out[...] = norm_forward(values, gain[...])[0].astype(BF16)
    mixed = dot(normed_out[...], weights[:, :mix_width])
    cos_table, sin_table = cosine[...], sine[...]
    scale = head_width ** (-0.5)
    width = group_size * head_width
    for head in range(group_size):
        part = slice(head * head_width, (head + 1) * head_width)
        queries_out[:, part] = (rotate(mixed[:, part], cos_table, sin_table) * scale).astype(BF16)
    keys_out[...] = rotate(mixed[:, width : width + head_width], cos_table, sin_table).astype(BF16)
    values_out[...] = mixed[:, width + head_width :].astype(BF16)
    allowed = visible(place_col, place_row, seg_col, seg_row)
    for head in range(group_size):
        part = slice(head * head_width, (head + 1) * head_width)
        scores = times_transposed(queries_out[:, part], keys_out[...])
        capped = jnp.where(allowed, soft_cap * jnp.tanh(scores / soft_cap), -jnp.inf)
        row_max = jnp.max(capped, axis=-1, keepdims=True)
        exp_scores = jnp.exp(capped - row_max)
        row_total = jnp.sum(exp_scores, axis=-1, keepdims=True)
        logsum_out[head] = row_max + jnp.log(row_total)
        context_out[:, part] = dot((exp_scores / row_total).astype(BF16), values_out[...]).astype(BF16)
    half = rows.shape[0] // 2
    other_out[...] = times_transposed(context_out[half:], weights[:, mix_width:]).astype(BF16)
    mine_out[...] = times_transposed(context_out[:half], weights[:, mix_width:])


def attend_back_kernel(
    group_size,
    head_width,
    slopes,
    weights,
    queries,
    keys,
    values,
    logsum,
    cosine,
    sine,
    place_col,
    place_row,
    seg_col,
    seg_row,
    mixed_out,
    mine_out,
    other_out,
):
    mix_width = (group_size + 2) * head_width
    width = group_size * head_width
    scale = head_width ** (-0.5)
    context_slope = dot(slopes[...], weights[:, mix_width:]).astype(BF16)
    cos_table, sin_table = cosine[...], -sine[...]
    allowed = visible(place_col, place_row, seg_col, seg_row)
    key_slope = jnp.zeros(keys.shape, F32)
    value_slope = jnp.zeros(values.shape, F32)
    for head in range(group_size):
        part = slice(head * head_width, (head + 1) * head_width)
        tanh_value = jnp.tanh(times_transposed(queries[:, part], keys[...]) / soft_cap)
        probs = jnp.where(allowed, jnp.exp(soft_cap * tanh_value - logsum[head]), 0.0)
        slope = context_slope[:, part]
        prob_slope = times_transposed(slope, values[...])
        value_slope += transposed(probs.astype(BF16), slope)
        inner_sum = jnp.sum(probs * prob_slope, axis=-1, keepdims=True)
        score_slope = (probs * (prob_slope - inner_sum) * (1.0 - tanh_value * tanh_value)).astype(BF16)
        query_slope = dot(score_slope, keys[...])
        key_slope += transposed(score_slope, queries[:, part])
        mixed_out[:, part] = rotate(query_slope * scale, cos_table, sin_table).astype(BF16)
    mixed_out[:, width : width + head_width] = rotate(key_slope, cos_table, sin_table).astype(BF16)
    mixed_out[:, width + head_width :] = value_slope.astype(BF16)
    half = slopes.shape[0] // 2
    other_out[...] = times_transposed(mixed_out[half:], weights[:, :mix_width]).astype(BF16)
    mine_out[...] = times_transposed(mixed_out[:half], weights[:, :mix_width])


root_two_pi = 0.7978845608028654
cubic = 0.044715


def gate_up_kernel(main, rows, weights, active_out, gate_out, up_out):
    result = dot(rows[...], weights[0])
    quarter = weights.shape[2] // 2
    bounds = [
        (slice(0, main), slice(main, 2 * main), slice(0, main)),
        (slice(2 * main, main + quarter), slice(main + quarter, 2 * quarter), slice(main, quarter)),
    ]
    for gate_part, up_part, part in bounds:
        gate, up = result[:, gate_part], result[:, up_part]
        square = gate * gate
        tanh_value = jnp.tanh(root_two_pi * gate * (1.0 + cubic * square))
        near = 0.5 * (1.0 + tanh_value)
        gelu = gate * near
        slope = near + 0.5 * gate * (1.0 - tanh_value * tanh_value) * root_two_pi * (
            1.0 + 3.0 * cubic * square
        )
        active_out[0, :, part] = (gelu * up).astype(BF16)
        gate_out[0, :, part] = (slope * up).astype(BF16)
        up_out[0, :, part] = gelu.astype(BF16)


def gate_up_call(rows, weights, main):
    count, width, columns = weights.shape
    height = rows.shape[0]
    quarter = columns // 2
    out_block = pl.BlockSpec((1, height, quarter), lambda i: (i, 0, 0))
    return pl.pallas_call(
        functools.partial(gate_up_kernel, main),
        grid=(count,),
        in_specs=[
            pl.BlockSpec((height, width), lambda i: (0, 0)),
            pl.BlockSpec((1, width, columns), lambda i: (i, 0, 0)),
        ],
        out_specs=[out_block] * 3,
        out_shape=[shape((count, height, quarter))] * 3,
        compiler_params=params,
    )(rows, weights)


def down_kernel(active, weights, *refs):
    out = refs[-1]
    total = times_transposed(active[0], weights[0])
    for place in range(1, active.shape[0]):
        total += times_transposed(active[place], weights[place])
    if len(refs) > 1:
        total += refs[0][...].astype(F32)
    out[...] = total.astype(out.dtype)


def down_call(active, weights, out_type, *received):
    count, height, quarter = active.shape
    width = weights.shape[1]
    tile = width // 3
    block = pl.BlockSpec((height, tile), lambda i: (0, i))
    return pl.pallas_call(
        down_kernel,
        grid=(3,),
        in_specs=[
            pl.BlockSpec((count, height, quarter), lambda i: (0, 0, 0)),
            pl.BlockSpec((count, tile, quarter), lambda i: (0, i, 0)),
        ]
        + [block] * len(received),
        out_specs=block,
        out_shape=shape((height, width), out_type),
        compiler_params=params,
    )(active, weights, *received)


def feed_back_kernel(main, slopes, down, gate_up, gate_factor, up_factor, slope_out, out, total):
    step = pl.program_id(0)
    active_slope = dot(slopes[...], down[0])
    quarter = active_slope.shape[1]
    gate_slope = (active_slope * gate_factor[0].astype(F32)).astype(BF16)
    up_slope = (active_slope * up_factor[0].astype(F32)).astype(BF16)
    slope_out[0] = jnp.concatenate(
        [gate_slope[:, :main], up_slope[:, :main], gate_slope[:, main:], up_slope[:, main:]], axis=1
    )
    product = times_transposed(slope_out[0], gate_up[0])

    @pl.when(step == 0)
    def _():
        total[...] = product

    @pl.when(step > 0)
    def _():
        total[...] += product

    @pl.when(step == pl.num_programs(0) - 1)
    def _():
        out[...] = total[...].astype(out.dtype)


def feed_back_call(slopes, down, gate_up, gate_factor, up_factor, main, out_type):
    height, width = slopes.shape
    count, _, columns = gate_up.shape
    quarter = columns // 2
    whole_block = pl.BlockSpec((height, width), lambda i: (0, 0))

    def each(rows, wide):
        return pl.BlockSpec((1, rows, wide), lambda i: (i, 0, 0))

    return pl.pallas_call(
        functools.partial(feed_back_kernel, main),
        grid=(count,),
        in_specs=[
            whole_block,
            each(width, quarter),
            each(width, columns),
            each(height, quarter),
            each(height, quarter),
        ],
        out_specs=[each(height, columns), whole_block],
        out_shape=[shape((count, height, columns)), shape((height, width), out_type)],
        scratch_shapes=[pltpu.VMEM((height, width), F32)],
        compiler_params=params,
    )(slopes, down, gate_up, gate_factor, up_factor)


def weight_slope_kernel(left_mine, left_other, right_mine, right_other, out):
    total = transposed(left_mine[...], right_mine[0]) + transposed(left_other[...], right_other[0])
    out[0] = total.astype(BF16)


def weight_slope_call(lefts, rights):
    height, width = lefts[0].shape
    count, _, columns = rights[0].shape
    tile = width // 3
    left_block = pl.BlockSpec((height, tile), lambda i, j: (0, j))
    right_block = pl.BlockSpec((1, height, columns), lambda i, j: (i, 0, 0))
    return pl.pallas_call(
        weight_slope_kernel,
        grid=(count, 3),
        in_specs=[left_block] * 2 + [right_block] * 2,
        out_specs=pl.BlockSpec((1, tile, columns), lambda i, j: (i, j, 0)),
        out_shape=shape((count, width, columns)),
        compiler_params=params,
    )(*lefts, *rights)


def gate_up_adam_kernel(main, depth, *refs):
    pieces, (weight, mean, power), outs = refs[:DEPTH], refs[DEPTH : DEPTH + 3], refs[DEPTH + 3 :]
    rest = pieces[0].shape[1] // 2 - main
    quarters = []
    for place in range(DEPTH):
        step = (place - depth[0]) % DEPTH
        value = pieces[0][...]
        for ahead in range(1, DEPTH):
            value = jnp.where(step == ahead, pieces[ahead][...], value)
        quarters.append(value.astype(F32))
    for slot in range(2):
        begin = 2 * main + slot * rest
        gradient = jnp.concatenate(
            [value[:, slot * main : (slot + 1) * main] for value in quarters]
            + [value[:, begin : begin + rest] for value in quarters],
            axis=1,
        )
        result = adam_step(weight[:, slot], gradient, mean[:, slot], power[:, slot])
        for out, value in zip(outs, (gradient,) + result[:3]):
            out[:, slot] = value


def gate_up_adam_call(depth, pieces, weight, mean, power, main):
    block, columns = pieces[0].shape
    tile = 24 if block % 32 else 32
    piece_block = pl.BlockSpec((tile, columns), lambda i, depth: (i, 0))
    weight_block = pl.BlockSpec((tile,) + weight.shape[1:], lambda i, depth: (i, 0, 0))
    return pl.pallas_call(
        functools.partial(gate_up_adam_kernel, main),
        grid_spec=pltpu.PrefetchScalarGridSpec(
            num_scalar_prefetch=1,
            grid=(block // tile,),
            in_specs=[piece_block] * DEPTH + [weight_block] * 3,
            out_specs=[weight_block] * 4,
        ),
        out_shape=[shape(weight.shape, F32)] * 4,
        compiler_params=params,
    )(depth.reshape(1), *pieces, weight, mean, power)


def make_device(side_size):
    def per_device(
        inputs,
        segments,
        cotangent,
        project_weight,
        output_weight,
        gate_up_weight,
        down_weight,
        norm_gains,
        project_mean,
        project_power,
        output_mean,
        output_power,
        gate_up_mean,
        gate_up_power,
        down_mean,
        down_power,
        gains_mean,
        gains_power,
    ):
        depth, side, row, core = (lax.axis_index(name) for name in ("z", "x", "y", "c"))
        own_rows, width = inputs.shape
        block = project_weight.shape[0]
        head_width = project_weight.shape[3]
        slots = project_weight.shape[2]
        group_size = slots - 2
        kv_local = project_weight.shape[1]
        mix_width = kv_local * slots * head_width
        context_width = output_weight.shape[0]
        hidden = down_weight.shape[0]
        quarter = hidden // DEPTH
        main = quarter // 128 * 128
        total_rows = 4 * own_rows
        seq_count = total_rows // SEQ

        def arrange(value):
            lead = value.shape[0]
            value = value.reshape(lead, DEPTH, side_size, block).transpose(0, 2, 1, 3)
            return value.reshape(lead, width)

        def unarrange(value):
            lead = value.shape[0]
            value = value.reshape(lead, side_size, DEPTH, block).transpose(0, 2, 1, 3)
            return value.reshape(lead, width)

        attend_own = jnp.concatenate(
            [project_weight.astype(BF16).reshape(block, mix_width), output_weight.astype(BF16).T],
            axis=1,
        )
        rows_own = arrange(inputs)

        def gather_sequence(value):
            mine = jnp.concatenate([value, swap(value, "y")], axis=0)
            return jnp.concatenate([mine, swap(mine, "c")], axis=0)

        def scatter_sequence(mine, other, *earlier):
            mine = mine + swap(other, "c").astype(F32)
            if earlier:
                mine = after(mine, *earlier)
            return mine[:own_rows] + swap(mine[own_rows:].astype(BF16), "y").astype(F32)

        def gather_group(value):
            mine = jnp.concatenate(
                [value] + [from_ahead(value, "z", DEPTH, step) for step in range(1, DEPTH)], axis=0
            )
            return mine, swap(mine, "c")

        def scatter_group(mine):
            total = mine[:own_rows]
            received = []
            for step in range(1, DEPTH):
                part = mine[step * own_rows : (step + 1) * own_rows].astype(BF16)
                received.append(from_ahead(part, "z", DEPTH, DEPTH - step))
                total = total + received[-1].astype(F32)
            return total, received[0]

        gains_parts = ordered(norm_gains, swap(norm_gains, "y"), row)
        gains_parts = ordered(gains_parts, swap(gains_parts, "c"), core)
        gains_own = gains_parts.transpose(2, 1, 0, 3).reshape(1, 4 * block).astype(BF16)
        attend_width = mix_width + context_width
        extra = 8
        attend_own = jnp.concatenate(
            [attend_own, jnp.pad(gains_own, ((0, extra - 1), (0, attend_width - 4 * block)))], axis=0
        )

        def quartered(weight):
            whole = weight[:, : DEPTH * main].reshape(-1, DEPTH, main).transpose(1, 0, 2)
            rest = weight[:, DEPTH * main :].reshape(-1, DEPTH, quarter - main).transpose(1, 0, 2)
            return whole, rest

        def unquartered(whole, rest):
            return jnp.concatenate(
                [
                    whole.transpose(1, 0, 2).reshape(-1, DEPTH * main),
                    rest.transpose(1, 0, 2).reshape(-1, DEPTH * (quarter - main)),
                ],
                axis=1,
            )

        def over_z(pieces):
            return [from_ahead(piece, "z", DEPTH, step + 1) for step, piece in enumerate(pieces)]

        def quarter_pieces(pieces):
            return [
                lax.dynamic_index_in_dim(pieces, (depth - step) % DEPTH, 0, keepdims=False)
                for step in range(DEPTH)
            ]

        def by_depth(received):
            result = jnp.zeros((DEPTH * block, received[0].shape[1]), BF16)
            for step in range(DEPTH):
                result = lax.dynamic_update_slice(
                    result, received[step], ((depth + step) % DEPTH * block, 0)
                )
            return result

        def over_x(piece):
            return [from_ahead(piece, "x", side_size, ahead) for ahead in range(1, side_size)]

        gate_whole, gate_rest = quartered(gate_up_weight[:, 0].astype(BF16))
        up_whole, up_rest = quartered(gate_up_weight[:, 1].astype(BF16))
        gate_up_pieces = quarter_pieces(
            jnp.concatenate([gate_whole, up_whole, gate_rest, up_rest], axis=2)
        )
        down_pieces = quarter_pieces(jnp.concatenate(quartered(down_weight.astype(BF16).T), axis=2))

        attend_sent, rows_sent, *gate_up_sent = gated([attend_own, rows_own, *gate_up_pieces[1:]])
        gate_up_own = over_z(gate_up_sent)
        attend_across = [[attend_sent] + over_x(attend_sent)]
        rows_row = swap(rows_sent, "y")

        rows_half = jnp.concatenate([rows_own, rows_row], axis=0)
        rows_half, *attend_sent = gated(
            [rows_half, attend_own, attend_own, attend_own], *attend_across[0][1:], *gate_up_own
        )
        rows_in = jnp.concatenate([rows_half, swap(rows_half, "c")], axis=0)
        gate_up_own = by_depth(gate_up_pieces[:1] + gate_up_own)
        gate_up_own = after(gate_up_own, rows_row, *attend_across[0][1:])
        full_gate_up = lax.all_gather(gate_up_own, ("y", "x"), axis=0, tiled=True)
        full_gate_up = full_gate_up.reshape(2, width, 2 * quarter)
        near_pieces = [
            from_ahead(attend_sent[0], "z", DEPTH, 1),
            from_ahead(attend_sent[2], "z", DEPTH, 3),
        ]

        far_sent, *near_sent = gated([attend_sent[1], *near_pieces], rows_in)
        far_piece = from_ahead(far_sent, "z", DEPTH, 2)
        near_across = [[piece] + over_x(piece) for piece in near_sent]

        far_sent, *down_sent = gated(
            [far_piece, *down_pieces[1:]], *near_across[0][1:], *near_across[1][1:]
        )
        attend_across += [near_across[0], [far_sent] + over_x(far_sent), near_across[1]]
        down_received = over_z(down_sent)
        down_own = after(by_depth(down_pieces[:1] + down_received), full_gate_up)
        full_down = lax.all_gather(down_own, ("y", "x"), axis=0, tiled=True).reshape(2, width, quarter)

        full_attend = jnp.zeros((side_size, DEPTH, block, attend_width), BF16)
        gains_all = jnp.zeros((side_size, DEPTH, 4, block), BF16)
        for step in range(DEPTH):
            for ahead in range(side_size):
                piece = attend_across[step][ahead]
                place = ((side + ahead) % side_size, (depth + step) % DEPTH, 0, 0)
                full_attend = lax.dynamic_update_slice(full_attend, piece[None, None, :block], place)
                gains_piece = piece[block : block + 1, : 4 * block].reshape(1, 1, 4, block)
                gains_all = lax.dynamic_update_slice(gains_all, gains_piece, place)
        full_attend = full_attend.reshape(width, attend_width)
        gains_all = gains_all.astype(F32).transpose(2, 0, 1, 3).reshape(4, width)

        residual_in = rows_own.astype(F32)
        factor_one = lax.rsqrt(jnp.mean(residual_in * residual_in, axis=-1, keepdims=True) + norm_eps)
        start = jnp.stack(
            [
                ((row ^ dr) * 2 + (core ^ dc)) * own_rows
                for dc in range(2)
                for dr in range(2)
            ]
        )
        order = (start[:, None] + jnp.arange(own_rows)[None, :]).reshape(total_rows)
        seg_parts = segments.reshape(2, 2, own_rows)
        seg_parts = rolled(rolled(seg_parts, row, 0), core, 1)
        seg_rows = seg_parts.transpose(1, 0, 2).reshape(total_rows)
        places = order
        half_width = head_width // 2
        frequency = rope_base ** (-2.0 * jnp.arange(half_width, dtype=F32) / head_width)
        angles = places.astype(F32)[:, None] * frequency[None, :]
        cosine_table, sine_table = jnp.cos(angles), jnp.sin(angles)
        tables = (
            cosine_table,
            sine_table,
            order[:, None],
            order[None, :],
            seg_rows[:, None],
            seg_rows[None, :],
        )
        rows_one, queries, key_vectors, value_rows, logsum, context_flat, mine, other = pl.pallas_call(
            functools.partial(attend_kernel, group_size, head_width),
            in_specs=whole(9),
            out_specs=whole(8),
            out_shape=[
                shape((total_rows, width)),
                shape((total_rows, context_width)),
                shape((total_rows, head_width)),
                shape((total_rows, head_width)),
                shape((group_size, total_rows, 1), F32),
                shape((total_rows, context_width)),
                shape((total_rows // 2, width), F32),
                shape((total_rows // 2, width)),
            ],
            compiler_params=params,
        )(rows_in, gains_all[:1], full_attend, *tables)
        attend_sum = scatter_sequence(mine, after(other, *down_received))
        post_one, factor_two = norm_forward(attend_sum, gains_all[1])
        hidden_state = residual_in + post_one
        normed_two, factor_three = norm_forward(hidden_state, gains_all[2])

        rows_two = gather_group(normed_two.astype(BF16))
        activated, gate_factor, up_factor = zip(
            *[gate_up_call(rows, full_gate_up, main) for rows in rows_two]
        )
        received = swap(down_call(activated[1], full_down, BF16), "c")
        feed_sum = scatter_group(down_call(activated[0], full_down, F32, received))[0]
        post_two, factor_four = norm_forward(feed_sum, gains_all[3])
        layer_output = unarrange((hidden_state + post_two).astype(BF16))

        upstream = arrange(cotangent).astype(F32)
        feed_slope, gain_four = norm_backward(feed_sum, factor_four, gains_all[3], upstream)
        feed_slope_rows = gather_group(feed_slope.astype(BF16))
        def ffn_total(left, right):
            return weight_slope_call(left, right).reshape(2 * width, -1)

        def reduce_ffn(total):
            return lax.psum_scatter(total, ("y", "x"), scatter_dimension=0, tiled=True)

        down_total = ffn_total(feed_slope_rows, activated)
        later_rows = gated(feed_slope_rows, down_total)
        backs = [
            feed_back_call(
                later_rows[place],
                full_down,
                full_gate_up,
                gate_factor[place],
                up_factor[place],
                main,
                (F32, BF16)[place],
            )
            for place in range(2)
        ]
        received = swap(backs[1][1], "c")
        normed_two_slope, first_received = scatter_group(backs[0][1] + received.astype(F32))

        def owned(pieces):
            return rolled(jnp.stack(pieces), (DEPTH - depth) % DEPTH, 0)

        down_pieces = quarter_pieces(reduce_ffn(down_total).reshape(DEPTH, block, quarter))
        gate_up_total = ffn_total(rows_two, gated([back[0] for back in backs], first_received))
        gate_up_mine = reduce_ffn(gate_up_total)

        hidden_part, gain_three = norm_backward(
            hidden_state, factor_three, gains_all[2], normed_two_slope
        )
        hidden_slope = upstream + hidden_part
        attend_slope, gain_two = norm_backward(attend_sum, factor_two, gains_all[1], hidden_slope)

        attend_slope = after(attend_slope, gate_up_total)

        slope_sent, *down_sent = gated([attend_slope.astype(BF16), *down_pieces[1:]])
        attend_slope_rows = gather_sequence(slope_sent)
        down_received = over_z(down_sent)
        down_parts = owned(down_pieces[:1] + down_received)
        down_grad = unquartered(down_parts[:, :, :main], down_parts[:, :, main:]).T.astype(F32)
        mixed_slope, mine, other = pl.pallas_call(
            functools.partial(attend_back_kernel, group_size, head_width),
            in_specs=whole(12),
            out_specs=whole(3),
            out_shape=[
                shape((total_rows, mix_width)),
                shape((total_rows // 2, width), F32),
                shape((total_rows // 2, width)),
            ],
            compiler_params=params,
        )(attend_slope_rows, full_attend, queries, key_vectors, value_rows, logsum, *tables)
        def gradient(left, right):
            total = transposed(left, right).astype(BF16)
            return total.reshape(side_size, DEPTH, block, right.shape[1])

        def side_parts(total):
            return [
                lax.dynamic_index_in_dim(total, (side + ahead) % side_size, 0, keepdims=False)
                for ahead in range(side_size)
            ]

        def over_side(parts):
            across = parts[0].astype(F32)
            for ahead in range(1, side_size):
                across = across + from_ahead(parts[ahead], "x", side_size, side_size - ahead).astype(F32)
            return across

        gate_up_pieces = quarter_pieces(gate_up_mine.reshape(DEPTH, block, 2 * quarter))
        project_parts = side_parts(gradient(rows_one, mixed_slope))
        sent = gated([*project_parts[1:], *gate_up_pieces[1:]], *down_received)
        gate_up_received = over_z(sent[side_size - 1 :])
        project_here = after(project_parts[0], *gate_up_received)
        project_across = over_side([project_here] + sent[: side_size - 1])
        normed_one_slope = scatter_sequence(mine, other)

        input_part, gain_one = norm_backward(residual_in, factor_one, gains_all[0], normed_one_slope)
        input_grad = unarrange(hidden_slope + input_part)

        gain_sum = jnp.stack([gain_one, gain_two, gain_three, gain_four], axis=0)
        lines = -(-4 * block // context_width)
        gain_sum = gain_sum.reshape(4, side_size, DEPTH, block).transpose(1, 2, 0, 3)
        gain_sum = gain_sum.reshape(side_size, DEPTH, 4 * block).astype(BF16)
        gain_sum = jnp.pad(gain_sum, ((0, 0), (0, 0), (0, lines * context_width - 4 * block)))
        gain_sum = jnp.pad(
            gain_sum.reshape(side_size, DEPTH, lines, context_width),
            ((0, 0), (0, 0), (0, extra - lines), (0, 0)),
        )
        output_total = jnp.concatenate(
            [gradient(attend_slope_rows, context_flat), gain_sum], axis=2
        )

        output_parts = side_parts(output_total)
        project_pieces = quarter_pieces(project_across.astype(BF16))
        project_received = over_z(gated(project_pieces[1:], *gate_up_received))
        output_sent = gated(output_parts[1:], project_across)
        output_across = over_side(output_parts[:1] + output_sent)
        output_pieces = quarter_pieces(output_across.astype(BF16))
        output_received = over_z(gated(output_pieces[1:], *project_received))
        gate_up_sent = gated([gate_up_pieces[0], *gate_up_received], project_received[0])
        gate_up_grad, gate_up_new, gate_up_mean_new, gate_up_power_new = gate_up_adam_call(
            depth, gate_up_sent, gate_up_weight, gate_up_mean, gate_up_power, main
        )
        output_received = gated(output_received, gate_up_grad)

        def own_sum(across, received):
            mine = lax.dynamic_index_in_dim(across, depth, 0, keepdims=False)
            for part in received:
                mine = mine + part.astype(F32)
            return mine

        project_grad = own_sum(project_across, project_received).reshape(project_weight.shape)
        output_mine = own_sum(output_across, output_received)
        output_grad = output_mine[:block].T
        gain_part = output_mine[block : block + lines].reshape(1, -1)[:, : 4 * block]
        gain_part = gain_part.reshape(4, 2, 2, norm_gains.shape[1]).transpose(1, 2, 0, 3)
        for axis, place in (("y", row), ("c", core)):
            parts = rolled(gain_part, place, 0)
            gain_part = parts[0] + swap(parts[1], axis)
        gains_grad = gain_part

        project_new, project_mean_new, project_power_new, unused_one = adam_step(
            project_weight, project_grad, project_mean, project_power
        )
        output_new, output_mean_new, output_power_new, unused_two = adam_step(
            output_weight, output_grad, output_mean, output_power
        )
        down_new, down_mean_new, down_power_new, unused_four = adam_step(
            down_weight, down_grad, down_mean, down_power
        )
        unused_five, gains_mean_new, gains_power_new, gains_step = adam_step(
            norm_gains, gains_grad, gains_mean, gains_power
        )
        return (
            layer_output,
            input_grad,
            project_grad,
            project_new,
            project_mean_new,
            project_power_new,
            output_grad,
            output_new,
            output_mean_new,
            output_power_new,
            gate_up_grad,
            gate_up_new,
            gate_up_mean_new,
            gate_up_power_new,
            down_grad,
            down_new,
            down_mean_new,
            down_power_new,
            gains_grad,
            gains_step,
            gains_mean_new,
            gains_power_new,
        )

    return per_device


def solution(mesh):
    side_size = mesh.shape["fsdp"] // DEPTH
    fine = Mesh(mesh.devices.reshape(DEPTH, side_size, 2, 2), ("z", "x", "y", "c"))
    fsdp = ("z", "x")
    tp = ("y", "c")
    both = fsdp + tp
    rows = P(both, None)
    project = P(fsdp, tp, None, None)
    across = P(tp, fsdp)
    gate_up = P(fsdp, None, tp)
    gains = P(None, both)
    in_specs = (
        (rows, P(fsdp), rows, project, across, gate_up, across, gains)
        + (project,) * 2
        + (across,) * 2
        + (gate_up,) * 2
        + (across,) * 2
        + (gains,) * 2
    )
    out_specs = (
        (rows, rows)
        + (project,) * 4
        + (across,) * 4
        + (gate_up,) * 4
        + (across,) * 4
        + (gains,) * 4
    )
    return jax.shard_map(
        make_device(side_size), mesh=fine, in_specs=in_specs, out_specs=out_specs, check_vma=False
    )
```

```python
import functools

import jax
import jax.numpy as jnp
from jax import lax
from jax.experimental import pallas as pl
from jax.experimental.pallas import tpu as pltpu
from jax.sharding import Mesh
from jax.sharding import PartitionSpec as P

SEQ = 512
DEPTH = 4

norm_eps = 1e-06
soft_cap = 50.0
rope_base = 10000.0
beta_first = 0.9
beta_second = 0.95
learn_rate = 0.02
decay_rate = 0.1
adam_eps = 1e-08
step_number = 3.0

F32 = jnp.float32
BF16 = jnp.bfloat16


def norm_forward(values, gain_vec):
    factor = lax.rsqrt(jnp.mean(values * values, axis=-1, keepdims=True) + norm_eps)
    return (values * factor * gain_vec, factor)


def norm_backward(values, factor, gain_vec, incoming):
    unit_rows = values * factor
    gain_part = jnp.sum(incoming * unit_rows, axis=0)
    scaled = incoming * gain_vec
    return (
        factor * (scaled - unit_rows * jnp.mean(scaled * unit_rows, axis=-1, keepdims=True)),
        gain_part,
    )


def rotate(values, cosine_table, sine_table):
    half_width = values.shape[-1] // 2
    first_half = values[:, :half_width]
    second_half = values[:, half_width:]
    return jnp.concatenate(
        [
            first_half * cosine_table - second_half * sine_table,
            second_half * cosine_table + first_half * sine_table,
        ],
        axis=-1,
    )


def adam_step(weight, gradient, mean_old, power_old):
    mean_new = beta_first * mean_old + (1.0 - beta_first) * gradient
    power_new = beta_second * power_old + (1.0 - beta_second) * gradient * gradient
    mean_hat = mean_new / (1.0 - beta_first**step_number)
    power_hat = power_new / (1.0 - beta_second**step_number)
    change = -learn_rate * (mean_hat / (jnp.sqrt(power_hat) + adam_eps) + decay_rate * weight)
    return (weight + change, mean_new, power_new, change)


def swap(value, axis):
    return lax.ppermute(value, axis, [(0, 1), (1, 0)])


def from_ahead(value, axis, size, step):
    return lax.ppermute(value, axis, [(j, (j - step) % size) for j in range(size)])


def after(value, *others):
    return lax.optimization_barrier((value,) + others)[0]


def gated(values, *others):
    values = list(values)
    return list(lax.optimization_barrier(tuple(values) + others)[: len(values)])


def ordered(own, other, place):
    straight = jnp.stack([own, other])
    return jnp.where(place == 0, straight, straight[::-1])


def rolled(value, place, axis):
    count = value.shape[axis]
    result = value
    for step in range(1, count):
        result = jnp.where(place == step, jnp.roll(value, -step, axis), result)
    return result


def transposed(left, right):
    return lax.dot_general(left, right, (((0,), (0,)), ((), ())), preferred_element_type=F32)


def times_transposed(left, right):
    return lax.dot_general(left, right, (((1,), (1,)), ((), ())), preferred_element_type=F32)


VMEM_LIMIT = 60 * 1024 * 1024
params = pltpu.CompilerParams(vmem_limit_bytes=VMEM_LIMIT)


def whole(count):
    return [pl.BlockSpec(memory_space=pltpu.VMEM)] * count


def shape(dims, dtype=BF16):
    return jax.ShapeDtypeStruct(dims, dtype)


def dot(left, right):
    return jnp.dot(left, right, preferred_element_type=F32)


def visible(place_col, place_row, seg_col, seg_row):
    return (seg_col[...] == seg_row[...]) & (place_row[...] <= place_col[...])


def attend_kernel(
    group_size,
    head_width,
    rows,
    gain,
    weights,
    cosine,
    sine,
    place_col,
    place_row,
    seg_col,
    seg_row,
    normed_out,
    queries_out,
    keys_out,
    values_out,
    logsum_out,
    context_out,
    mine_out,
    other_out,
):
    mix_width = (group_size + 2) * head_width
    values = rows[...].astype(F32)
    normed_out[...] = norm_forward(values, gain[...])[0].astype(BF16)
    mixed = dot(normed_out[...], weights[:, :mix_width])
    cos_table, sin_table = cosine[...], sine[...]
    scale = head_width ** (-0.5)
    width = group_size * head_width
    for head in range(group_size):
        part = slice(head * head_width, (head + 1) * head_width)
        queries_out[:, part] = (rotate(mixed[:, part], cos_table, sin_table) * scale).astype(BF16)
    keys_out[...] = rotate(mixed[:, width : width + head_width], cos_table, sin_table).astype(BF16)
    values_out[...] = mixed[:, width + head_width :].astype(BF16)
    allowed = visible(place_col, place_row, seg_col, seg_row)
    for head in range(group_size):
        part = slice(head * head_width, (head + 1) * head_width)
        scores = times_transposed(queries_out[:, part], keys_out[...])
        capped = jnp.where(allowed, soft_cap * jnp.tanh(scores / soft_cap), -jnp.inf)
        row_max = jnp.max(capped, axis=-1, keepdims=True)
        exp_scores = jnp.exp(capped - row_max)
        row_total = jnp.sum(exp_scores, axis=-1, keepdims=True)
        logsum_out[head] = row_max + jnp.log(row_total)
        context_out[:, part] = dot((exp_scores / row_total).astype(BF16), values_out[...]).astype(BF16)
    half = rows.shape[0] // 2
    other_out[...] = times_transposed(context_out[half:], weights[:, mix_width:]).astype(BF16)
    mine_out[...] = times_transposed(context_out[:half], weights[:, mix_width:])


def attend_back_kernel(
    group_size,
    head_width,
    slopes,
    weights,
    queries,
    keys,
    values,
    logsum,
    cosine,
    sine,
    place_col,
    place_row,
    seg_col,
    seg_row,
    mixed_out,
    mine_out,
    other_out,
):
    mix_width = (group_size + 2) * head_width
    width = group_size * head_width
    scale = head_width ** (-0.5)
    context_slope = dot(slopes[...], weights[:, mix_width:]).astype(BF16)
    cos_table, sin_table = cosine[...], -sine[...]
    allowed = visible(place_col, place_row, seg_col, seg_row)
    key_slope = jnp.zeros(keys.shape, F32)
    value_slope = jnp.zeros(values.shape, F32)
    for head in range(group_size):
        part = slice(head * head_width, (head + 1) * head_width)
        tanh_value = jnp.tanh(times_transposed(queries[:, part], keys[...]) / soft_cap)
        probs = jnp.where(allowed, jnp.exp(soft_cap * tanh_value - logsum[head]), 0.0)
        slope = context_slope[:, part]
        prob_slope = times_transposed(slope, values[...])
        value_slope += transposed(probs.astype(BF16), slope)
        inner_sum = jnp.sum(probs * prob_slope, axis=-1, keepdims=True)
        score_slope = (probs * (prob_slope - inner_sum) * (1.0 - tanh_value * tanh_value)).astype(BF16)
        query_slope = dot(score_slope, keys[...])
        key_slope += transposed(score_slope, queries[:, part])
        mixed_out[:, part] = rotate(query_slope * scale, cos_table, sin_table).astype(BF16)
    mixed_out[:, width : width + head_width] = rotate(key_slope, cos_table, sin_table).astype(BF16)
    mixed_out[:, width + head_width :] = value_slope.astype(BF16)
    half = slopes.shape[0] // 2
    other_out[...] = times_transposed(mixed_out[half:], weights[:, :mix_width]).astype(BF16)
    mine_out[...] = times_transposed(mixed_out[:half], weights[:, :mix_width])


root_two_pi = 0.7978845608028654
cubic = 0.044715


def gate_up_kernel(main, rows, weights, active_out, gate_out, up_out):
    result = dot(rows[...], weights[0])
    quarter = weights.shape[2] // 2
    bounds = [
        (slice(0, main), slice(main, 2 * main), slice(0, main)),
        (slice(2 * main, main + quarter), slice(main + quarter, 2 * quarter), slice(main, quarter)),
    ]
    for gate_part, up_part, part in bounds:
        gate, up = result[:, gate_part], result[:, up_part]
        square = gate * gate
        tanh_value = jnp.tanh(root_two_pi * gate * (1.0 + cubic * square))
        near = 0.5 * (1.0 + tanh_value)
        gelu = gate * near
        slope = near + 0.5 * gate * (1.0 - tanh_value * tanh_value) * root_two_pi * (
            1.0 + 3.0 * cubic * square
        )
        active_out[0, :, part] = (gelu * up).astype(BF16)
        gate_out[0, :, part] = (slope * up).astype(BF16)
        up_out[0, :, part] = gelu.astype(BF16)


def gate_up_call(rows, weights, main):
    count, width, columns = weights.shape
    height = rows.shape[0]
    quarter = columns // 2
    out_block = pl.BlockSpec((1, height, quarter), lambda i: (i, 0, 0))
    return pl.pallas_call(
        functools.partial(gate_up_kernel, main),
        grid=(count,),
        in_specs=[
            pl.BlockSpec((height, width), lambda i: (0, 0)),
            pl.BlockSpec((1, width, columns), lambda i: (i, 0, 0)),
        ],
        out_specs=[out_block] * 3,
        out_shape=[shape((count, height, quarter))] * 3,
        compiler_params=params,
    )(rows, weights)


def down_kernel(active, weights, *refs):
    out = refs[-1]
    total = times_transposed(active[0], weights[0])
    for place in range(1, active.shape[0]):
        total += times_transposed(active[place], weights[place])
    if len(refs) > 1:
        total += refs[0][...].astype(F32)
    out[...] = total.astype(out.dtype)


def down_call(active, weights, out_type, *received):
    count, height, quarter = active.shape
    width = weights.shape[1]
    tile = width // 3
    block = pl.BlockSpec((height, tile), lambda i: (0, i))
    return pl.pallas_call(
        down_kernel,
        grid=(3,),
        in_specs=[
            pl.BlockSpec((count, height, quarter), lambda i: (0, 0, 0)),
            pl.BlockSpec((count, tile, quarter), lambda i: (0, i, 0)),
        ]
        + [block] * len(received),
        out_specs=block,
        out_shape=shape((height, width), out_type),
        compiler_params=params,
    )(active, weights, *received)


def feed_back_kernel(main, slopes, down, gate_up, gate_factor, up_factor, slope_out, out, total):
    step = pl.program_id(0)
    active_slope = dot(slopes[...], down[0])
    quarter = active_slope.shape[1]
    gate_slope = (active_slope * gate_factor[0].astype(F32)).astype(BF16)
    up_slope = (active_slope * up_factor[0].astype(F32)).astype(BF16)
    slope_out[0] = jnp.concatenate(
        [gate_slope[:, :main], up_slope[:, :main], gate_slope[:, main:], up_slope[:, main:]], axis=1
    )
    product = times_transposed(slope_out[0], gate_up[0])

    @pl.when(step == 0)
    def _():
        total[...] = product

    @pl.when(step > 0)
    def _():
        total[...] += product

    @pl.when(step == pl.num_programs(0) - 1)
    def _():
        out[...] = total[...].astype(out.dtype)


def feed_back_call(slopes, down, gate_up, gate_factor, up_factor, main, out_type):
    height, width = slopes.shape
    count, _, columns = gate_up.shape
    quarter = columns // 2
    whole_block = pl.BlockSpec((height, width), lambda i: (0, 0))

    def each(rows, wide):
        return pl.BlockSpec((1, rows, wide), lambda i: (i, 0, 0))

    return pl.pallas_call(
        functools.partial(feed_back_kernel, main),
        grid=(count,),
        in_specs=[
            whole_block,
            each(width, quarter),
            each(width, columns),
            each(height, quarter),
            each(height, quarter),
        ],
        out_specs=[each(height, columns), whole_block],
        out_shape=[shape((count, height, columns)), shape((height, width), out_type)],
        scratch_shapes=[pltpu.VMEM((height, width), F32)],
        compiler_params=params,
    )(slopes, down, gate_up, gate_factor, up_factor)


def weight_slope_kernel(left_mine, left_other, right_mine, right_other, out):
    total = transposed(left_mine[...], right_mine[0]) + transposed(left_other[...], right_other[0])
    out[0] = total.astype(BF16)


def weight_slope_call(lefts, rights):
    height, width = lefts[0].shape
    count, _, columns = rights[0].shape
    tile = width // 3
    left_block = pl.BlockSpec((height, tile), lambda i, j: (0, j))
    right_block = pl.BlockSpec((1, height, columns), lambda i, j: (i, 0, 0))
    return pl.pallas_call(
        weight_slope_kernel,
        grid=(count, 3),
        in_specs=[left_block] * 2 + [right_block] * 2,
        out_specs=pl.BlockSpec((1, tile, columns), lambda i, j: (i, j, 0)),
        out_shape=shape((count, width, columns)),
        compiler_params=params,
    )(*lefts, *rights)


def gate_up_adam_kernel(main, depth, *refs):
    pieces, (weight, mean, power), outs = refs[:DEPTH], refs[DEPTH : DEPTH + 3], refs[DEPTH + 3 :]
    rest = pieces[0].shape[1] // 2 - main
    quarters = []
    for place in range(DEPTH):
        step = (place - depth[0]) % DEPTH
        value = pieces[0][...]
        for ahead in range(1, DEPTH):
            value = jnp.where(step == ahead, pieces[ahead][...], value)
        quarters.append(value.astype(F32))
    for slot in range(2):
        begin = 2 * main + slot * rest
        gradient = jnp.concatenate(
            [value[:, slot * main : (slot + 1) * main] for value in quarters]
            + [value[:, begin : begin + rest] for value in quarters],
            axis=1,
        )
        result = adam_step(weight[:, slot], gradient, mean[:, slot], power[:, slot])
        for out, value in zip(outs, (gradient,) + result[:3]):
            out[:, slot] = value


def gate_up_adam_call(depth, pieces, weight, mean, power, main):
    block, columns = pieces[0].shape
    tile = 24 if block % 32 else 32
    piece_block = pl.BlockSpec((tile, columns), lambda i, depth: (i, 0))
    weight_block = pl.BlockSpec((tile,) + weight.shape[1:], lambda i, depth: (i, 0, 0))
    return pl.pallas_call(
        functools.partial(gate_up_adam_kernel, main),
        grid_spec=pltpu.PrefetchScalarGridSpec(
            num_scalar_prefetch=1,
            grid=(block // tile,),
            in_specs=[piece_block] * DEPTH + [weight_block] * 3,
            out_specs=[weight_block] * 4,
        ),
        out_shape=[shape(weight.shape, F32)] * 4,
        compiler_params=params,
    )(depth.reshape(1), *pieces, weight, mean, power)


def make_device(side_size):
    def per_device(
        inputs,
        segments,
        cotangent,
        project_weight,
        output_weight,
        gate_up_weight,
        down_weight,
        norm_gains,
        project_mean,
        project_power,
        output_mean,
        output_power,
        gate_up_mean,
        gate_up_power,
        down_mean,
        down_power,
        gains_mean,
        gains_power,
    ):
        depth, side, row, core = (lax.axis_index(name) for name in ("z", "x", "y", "c"))
        own_rows, width = inputs.shape
        block = project_weight.shape[0]
        head_width = project_weight.shape[3]
        slots = project_weight.shape[2]
        group_size = slots - 2
        kv_local = project_weight.shape[1]
        mix_width = kv_local * slots * head_width
        context_width = output_weight.shape[0]
        hidden = down_weight.shape[0]
        quarter = hidden // DEPTH
        main = quarter // 128 * 128
        total_rows = 4 * own_rows
        seq_count = total_rows // SEQ

        def arrange(value):
            lead = value.shape[0]
            value = value.reshape(lead, DEPTH, side_size, block).transpose(0, 2, 1, 3)
            return value.reshape(lead, width)

        def unarrange(value):
            lead = value.shape[0]
            value = value.reshape(lead, side_size, DEPTH, block).transpose(0, 2, 1, 3)
            return value.reshape(lead, width)

        attend_own = jnp.concatenate(
            [project_weight.astype(BF16).reshape(block, mix_width), output_weight.astype(BF16).T],
            axis=1,
        )
        rows_own = arrange(inputs)

        def gather_sequence(value):
            mine = jnp.concatenate([value, swap(value, "y")], axis=0)
            return jnp.concatenate([mine, swap(mine, "c")], axis=0)

        def scatter_sequence(mine, other, *earlier):
            mine = mine + swap(other, "c").astype(F32)
            if earlier:
                mine = after(mine, *earlier)
            return mine[:own_rows] + swap(mine[own_rows:].astype(BF16), "y").astype(F32)

        def gather_group(value):
            mine = jnp.concatenate(
                [value] + [from_ahead(value, "z", DEPTH, step) for step in range(1, DEPTH)], axis=0
            )
            return mine, swap(mine, "c")

        def scatter_group(mine):
            total = mine[:own_rows]
            for step in range(1, DEPTH):
                part = mine[step * own_rows : (step + 1) * own_rows].astype(BF16)
                total = total + from_ahead(part, "z", DEPTH, DEPTH - step).astype(F32)
            return total

        gains_parts = ordered(norm_gains, swap(norm_gains, "y"), row)
        gains_parts = ordered(gains_parts, swap(gains_parts, "c"), core)
        gains_parts = gains_parts.transpose(2, 1, 0, 3).reshape(1, 4 * block)
        gains_high = lax.optimization_barrier(gains_parts.astype(BF16))
        gains_low = (gains_parts - gains_high.astype(F32)).astype(BF16)
        attend_width = mix_width + context_width
        extra = 8
        attend_own = jnp.concatenate(
            [
                attend_own,
                jnp.pad(
                    jnp.concatenate([gains_high, gains_low], axis=0),
                    ((0, extra - 2), (0, attend_width - 4 * block)),
                ),
            ],
            axis=0,
        )

        def quartered(weight):
            whole = weight[:, : DEPTH * main].reshape(-1, DEPTH, main).transpose(1, 0, 2)
            rest = weight[:, DEPTH * main :].reshape(-1, DEPTH, quarter - main).transpose(1, 0, 2)
            return whole, rest

        def unquartered(whole, rest):
            return jnp.concatenate(
                [
                    whole.transpose(1, 0, 2).reshape(-1, DEPTH * main),
                    rest.transpose(1, 0, 2).reshape(-1, DEPTH * (quarter - main)),
                ],
                axis=1,
            )

        def over_z(pieces):
            return [from_ahead(piece, "z", DEPTH, step + 1) for step, piece in enumerate(pieces)]

        def quarter_pieces(pieces):
            return [
                lax.dynamic_index_in_dim(pieces, (depth - step) % DEPTH, 0, keepdims=False)
                for step in range(DEPTH)
            ]

        def by_depth(received):
            result = jnp.zeros((DEPTH * block, received[0].shape[1]), BF16)
            for step in range(DEPTH):
                result = lax.dynamic_update_slice(
                    result, received[step], ((depth + step) % DEPTH * block, 0)
                )
            return result

        def over_x(piece):
            return [from_ahead(piece, "x", side_size, ahead) for ahead in range(1, side_size)]

        gate_whole, gate_rest = quartered(gate_up_weight[:, 0].astype(BF16))
        up_whole, up_rest = quartered(gate_up_weight[:, 1].astype(BF16))
        gate_up_pieces = quarter_pieces(
            jnp.concatenate([gate_whole, up_whole, gate_rest, up_rest], axis=2)
        )
        down_pieces = quarter_pieces(jnp.concatenate(quartered(down_weight.astype(BF16).T), axis=2))

        attend_sent, rows_sent, *down_sent = gated([attend_own, rows_own, *down_pieces[1:]])
        down_received = over_z(down_sent)
        attend_across = [[attend_sent] + over_x(attend_sent)]
        rows_row = swap(rows_sent, "y")

        rows_half = jnp.concatenate([rows_own, rows_row], axis=0)
        rows_half, *attend_sent = gated(
            [rows_half, attend_own, attend_own, attend_own], *attend_across[0][1:], *down_received
        )
        rows_in = jnp.concatenate([rows_half, swap(rows_half, "c")], axis=0)
        down_own = by_depth(down_pieces[:1] + down_received)
        down_own = after(down_own, rows_row, *attend_across[0][1:])
        full_down = lax.all_gather(down_own, ("y", "x"), axis=0, tiled=True).reshape(2, width, quarter)
        near_pieces = [
            from_ahead(attend_sent[0], "z", DEPTH, 1),
            from_ahead(attend_sent[2], "z", DEPTH, 3),
        ]

        far_sent, *near_sent = gated([attend_sent[1], *near_pieces], rows_in)
        far_piece = from_ahead(far_sent, "z", DEPTH, 2)
        near_across = [[piece] + over_x(piece) for piece in near_sent]

        far_sent, *gate_up_sent = gated(
            [far_piece, *gate_up_pieces[1:]], *near_across[0][1:], *near_across[1][1:]
        )
        attend_across += [near_across[0], [far_sent] + over_x(far_sent), near_across[1]]
        gate_up_received = over_z(gate_up_sent)
        gate_up_own = by_depth(gate_up_pieces[:1] + gate_up_received)
        gate_up_own = after(gate_up_own, full_down, *attend_across[2][1:])
        full_gate_up = lax.all_gather(gate_up_own, ("y", "x"), axis=0, tiled=True)
        full_gate_up = full_gate_up.reshape(2, width, 2 * quarter)

        full_attend = jnp.zeros((side_size, DEPTH, block, attend_width), BF16)
        gains_all = jnp.zeros((side_size, DEPTH, 4, block), F32)
        for step in range(DEPTH):
            for ahead in range(side_size):
                piece = attend_across[step][ahead]
                place = ((side + ahead) % side_size, (depth + step) % DEPTH, 0, 0)
                full_attend = lax.dynamic_update_slice(full_attend, piece[None, None, :block], place)
                gains_pair = piece[block : block + 2, : 4 * block].astype(F32)
                gains_piece = (gains_pair[0] + gains_pair[1]).reshape(1, 1, 4, block)
                gains_all = lax.dynamic_update_slice(gains_all, gains_piece, place)
        full_attend = full_attend.reshape(width, attend_width)
        gains_all = gains_all.transpose(2, 0, 1, 3).reshape(4, width)

        residual_in = rows_own.astype(F32)
        factor_one = lax.rsqrt(jnp.mean(residual_in * residual_in, axis=-1, keepdims=True) + norm_eps)
        start = jnp.stack(
            [
                ((row ^ dr) * 2 + (core ^ dc)) * own_rows
                for dc in range(2)
                for dr in range(2)
            ]
        )
        order = (start[:, None] + jnp.arange(own_rows)[None, :]).reshape(total_rows)
        seg_parts = segments.reshape(2, 2, own_rows)
        seg_parts = rolled(rolled(seg_parts, row, 0), core, 1)
        seg_rows = seg_parts.transpose(1, 0, 2).reshape(total_rows)
        places = order
        half_width = head_width // 2
        frequency = rope_base ** (-2.0 * jnp.arange(half_width, dtype=F32) / head_width)
        angles = places.astype(F32)[:, None] * frequency[None, :]
        cosine_table, sine_table = jnp.cos(angles), jnp.sin(angles)
        tables = (
            cosine_table,
            sine_table,
            order[:, None],
            order[None, :],
            seg_rows[:, None],
            seg_rows[None, :],
        )
        rows_one, queries, key_vectors, value_rows, logsum, context_flat, mine, other = pl.pallas_call(
            functools.partial(attend_kernel, group_size, head_width),
            in_specs=whole(9),
            out_specs=whole(8),
            out_shape=[
                shape((total_rows, width)),
                shape((total_rows, context_width)),
                shape((total_rows, head_width)),
                shape((total_rows, head_width)),
                shape((group_size, total_rows, 1), F32),
                shape((total_rows, context_width)),
                shape((total_rows // 2, width), F32),
                shape((total_rows // 2, width)),
            ],
            compiler_params=params,
        )(rows_in, gains_all[:1], full_attend, *tables)
        attend_sum = scatter_sequence(mine, other)
        post_one, factor_two = norm_forward(attend_sum, gains_all[1])
        hidden_state = residual_in + post_one
        normed_two, factor_three = norm_forward(hidden_state, gains_all[2])

        rows_two = gather_group(after(normed_two.astype(BF16), *gate_up_received))
        activated, gate_factor, up_factor = zip(
            *[gate_up_call(rows, full_gate_up, main) for rows in rows_two]
        )
        received = swap(down_call(activated[1], full_down, BF16), "c")
        feed_sum = scatter_group(down_call(activated[0], full_down, F32, received))
        post_two, factor_four = norm_forward(feed_sum, gains_all[3])
        layer_output = unarrange((hidden_state + post_two).astype(BF16))

        upstream = arrange(cotangent).astype(F32)
        feed_slope, gain_four = norm_backward(feed_sum, factor_four, gains_all[3], upstream)
        feed_slope_rows = gather_group(feed_slope.astype(BF16))
        def ffn_total(left, right):
            return weight_slope_call(left, right).reshape(2 * width, -1)

        def reduce_ffn(total):
            return lax.psum_scatter(total, ("y", "x"), scatter_dimension=0, tiled=True)

        down_total = ffn_total(feed_slope_rows, activated)
        later_rows = gated(feed_slope_rows, down_total)
        backs = [
            feed_back_call(
                later_rows[place],
                full_down,
                full_gate_up,
                gate_factor[place],
                up_factor[place],
                main,
                (F32, BF16)[place],
            )
            for place in range(2)
        ]
        received = swap(backs[1][1], "c")
        normed_two_slope = scatter_group(backs[0][1] + received.astype(F32))

        def owned(pieces):
            return rolled(jnp.stack(pieces), (DEPTH - depth) % DEPTH, 0)

        down_pieces = quarter_pieces(reduce_ffn(down_total).reshape(DEPTH, block, quarter))
        gate_up_total = ffn_total(rows_two, gated([back[0] for back in backs], received))
        gate_up_mine = reduce_ffn(gate_up_total)

        hidden_part, gain_three = norm_backward(
            hidden_state, factor_three, gains_all[2], normed_two_slope
        )
        hidden_slope = upstream + hidden_part
        attend_slope, gain_two = norm_backward(attend_sum, factor_two, gains_all[1], hidden_slope)

        attend_slope = after(attend_slope, gate_up_total)

        slope_sent, *down_sent = gated([attend_slope.astype(BF16), *down_pieces[1:]])
        attend_slope_rows = gather_sequence(slope_sent)
        down_received = over_z(down_sent)
        down_parts = owned(down_pieces[:1] + down_received)
        down_grad = unquartered(down_parts[:, :, :main], down_parts[:, :, main:]).T.astype(F32)
        mixed_slope, mine, other = pl.pallas_call(
            functools.partial(attend_back_kernel, group_size, head_width),
            in_specs=whole(12),
            out_specs=whole(3),
            out_shape=[
                shape((total_rows, mix_width)),
                shape((total_rows // 2, width), F32),
                shape((total_rows // 2, width)),
            ],
            compiler_params=params,
        )(attend_slope_rows, full_attend, queries, key_vectors, value_rows, logsum, *tables)
        def gradient(left, right):
            total = transposed(left, right).astype(BF16)
            return total.reshape(side_size, DEPTH, block, right.shape[1])

        def side_parts(total):
            return [
                lax.dynamic_index_in_dim(total, (side + ahead) % side_size, 0, keepdims=False)
                for ahead in range(side_size)
            ]

        def over_side(parts):
            across = parts[0].astype(F32)
            for ahead in range(1, side_size):
                across = across + from_ahead(parts[ahead], "x", side_size, side_size - ahead).astype(F32)
            return across

        gate_up_pieces = quarter_pieces(gate_up_mine.reshape(DEPTH, block, 2 * quarter))
        project_parts = side_parts(gradient(rows_one, mixed_slope))
        sent = gated([*project_parts[1:], *gate_up_pieces[1:]], *down_received)
        gate_up_received = over_z(sent[side_size - 1 :])
        project_here = after(project_parts[0], *gate_up_received)
        project_across = over_side([project_here] + sent[: side_size - 1])
        normed_one_slope = scatter_sequence(mine, other)

        input_part, gain_one = norm_backward(residual_in, factor_one, gains_all[0], normed_one_slope)
        input_grad = unarrange(hidden_slope + input_part)

        gain_sum = jnp.stack([gain_one, gain_two, gain_three, gain_four], axis=0)
        lines = -(-4 * block // context_width)
        gain_sum = gain_sum.reshape(4, side_size, DEPTH, block).transpose(1, 2, 0, 3)
        gain_sum = gain_sum.reshape(side_size, DEPTH, 4 * block).astype(BF16)
        gain_sum = jnp.pad(gain_sum, ((0, 0), (0, 0), (0, lines * context_width - 4 * block)))
        gain_sum = jnp.pad(
            gain_sum.reshape(side_size, DEPTH, lines, context_width),
            ((0, 0), (0, 0), (0, extra - lines), (0, 0)),
        )
        context_later = after(context_flat, gate_up_received[0])
        output_total = jnp.concatenate(
            [gradient(attend_slope_rows, context_later), gain_sum], axis=2
        )

        output_parts = side_parts(output_total)
        project_pieces = quarter_pieces(project_across.astype(BF16))
        project_received = over_z(gated(project_pieces[1:], *gate_up_received))
        output_sent = gated(output_parts[1:], project_across)
        output_across = over_side(output_parts[:1] + output_sent)
        output_pieces = quarter_pieces(output_across.astype(BF16))
        output_received = over_z(gated(output_pieces[1:], *project_received))
        gate_up_sent = gated([gate_up_pieces[0], *gate_up_received], project_received[0])
        gate_up_grad, gate_up_new, gate_up_mean_new, gate_up_power_new = gate_up_adam_call(
            depth, gate_up_sent, gate_up_weight, gate_up_mean, gate_up_power, main
        )
        output_received = gated(output_received, gate_up_grad)

        def own_sum(across, received):
            mine = lax.dynamic_index_in_dim(across, depth, 0, keepdims=False)
            for part in received:
                mine = mine + part.astype(F32)
            return mine

        project_grad = own_sum(project_across, project_received).reshape(project_weight.shape)
        output_mine = own_sum(output_across, output_received)
        output_grad = output_mine[:block].T
        gain_part = output_mine[block : block + lines].reshape(1, -1)[:, : 4 * block]
        gain_part = gain_part.reshape(4, 2, 2, norm_gains.shape[1]).transpose(1, 2, 0, 3)
        for axis, place in (("y", row), ("c", core)):
            parts = rolled(gain_part, place, 0)
            gain_part = parts[0] + swap(parts[1], axis)
        gains_grad = gain_part

        project_new, project_mean_new, project_power_new, unused_one = adam_step(
            project_weight, project_grad, project_mean, project_power
        )
        output_new, output_mean_new, output_power_new, unused_two = adam_step(
            output_weight, output_grad, output_mean, output_power
        )
        down_grad = after(down_grad, project_received[0])
        down_new, down_mean_new, down_power_new, unused_four = adam_step(
            down_weight, down_grad, down_mean, down_power
        )
        unused_five, gains_mean_new, gains_power_new, gains_step = adam_step(
            norm_gains, gains_grad, gains_mean, gains_power
        )
        return (
            layer_output,
            input_grad,
            project_grad,
            project_new,
            project_mean_new,
            project_power_new,
            output_grad,
            output_new,
            output_mean_new,
            output_power_new,
            gate_up_grad,
            gate_up_new,
            gate_up_mean_new,
            gate_up_power_new,
            down_grad,
            down_new,
            down_mean_new,
            down_power_new,
            gains_grad,
            gains_step,
            gains_mean_new,
            gains_power_new,
        )

    return per_device


def solution(mesh):
    side_size = mesh.shape["fsdp"] // DEPTH
    fine = Mesh(mesh.devices.reshape(DEPTH, side_size, 2, 2), ("z", "x", "y", "c"))
    fsdp = ("z", "x")
    tp = ("y", "c")
    both = fsdp + tp
    rows = P(both, None)
    project = P(fsdp, tp, None, None)
    across = P(tp, fsdp)
    gate_up = P(fsdp, None, tp)
    gains = P(None, both)
    in_specs = (
        (rows, P(fsdp), rows, project, across, gate_up, across, gains)
        + (project,) * 2
        + (across,) * 2
        + (gate_up,) * 2
        + (across,) * 2
        + (gains,) * 2
    )
    out_specs = (
        (rows, rows)
        + (project,) * 4
        + (across,) * 4
        + (gate_up,) * 4
        + (across,) * 4
        + (gains,) * 4
    )
    return jax.shard_map(
        make_device(side_size), mesh=fine, in_specs=in_specs, out_specs=out_specs, check_vma=False
    )
```

```python
import functools

import jax
import jax.numpy as jnp
from jax import lax
from jax.experimental import pallas as pl
from jax.experimental.pallas import tpu as pltpu
from jax.sharding import Mesh
from jax.sharding import PartitionSpec as P

SEQ = 512
DEPTH = 4

norm_eps = 1e-06
soft_cap = 50.0
rope_base = 10000.0
beta_first = 0.9
beta_second = 0.95
learn_rate = 0.02
decay_rate = 0.1
adam_eps = 1e-08
step_number = 3.0

F32 = jnp.float32
BF16 = jnp.bfloat16


def norm_forward(values, gain_vec):
    factor = lax.rsqrt(jnp.mean(values * values, axis=-1, keepdims=True) + norm_eps)
    return (values * factor * gain_vec, factor)


def norm_backward(values, factor, gain_vec, incoming):
    unit_rows = values * factor
    gain_part = jnp.sum(incoming * unit_rows, axis=0)
    scaled = incoming * gain_vec
    return (
        factor * (scaled - unit_rows * jnp.mean(scaled * unit_rows, axis=-1, keepdims=True)),
        gain_part,
    )


def rotate(values, cosine_table, sine_table):
    half_width = values.shape[-1] // 2
    first_half = values[:, :half_width]
    second_half = values[:, half_width:]
    return jnp.concatenate(
        [
            first_half * cosine_table - second_half * sine_table,
            second_half * cosine_table + first_half * sine_table,
        ],
        axis=-1,
    )


def adam_step(weight, gradient, mean_old, power_old):
    mean_new = beta_first * mean_old + (1.0 - beta_first) * gradient
    power_new = beta_second * power_old + (1.0 - beta_second) * gradient * gradient
    mean_hat = mean_new / (1.0 - beta_first**step_number)
    power_hat = power_new / (1.0 - beta_second**step_number)
    change = -learn_rate * (mean_hat / (jnp.sqrt(power_hat) + adam_eps) + decay_rate * weight)
    return (weight + change, mean_new, power_new, change)


def swap(value, axis):
    return lax.ppermute(value, axis, [(0, 1), (1, 0)])


def from_ahead(value, axis, size, step):
    return lax.ppermute(value, axis, [(j, (j - step) % size) for j in range(size)])


def after(value, *others):
    return lax.optimization_barrier((value,) + others)[0]


def gated(values, *others):
    values = list(values)
    return list(lax.optimization_barrier(tuple(values) + others)[: len(values)])


def ordered(own, other, place):
    straight = jnp.stack([own, other])
    return jnp.where(place == 0, straight, straight[::-1])


def rolled(value, place, axis):
    count = value.shape[axis]
    result = value
    for step in range(1, count):
        result = jnp.where(place == step, jnp.roll(value, -step, axis), result)
    return result


def transposed(left, right):
    return lax.dot_general(left, right, (((0,), (0,)), ((), ())), preferred_element_type=F32)


def times_transposed(left, right):
    return lax.dot_general(left, right, (((1,), (1,)), ((), ())), preferred_element_type=F32)


VMEM_LIMIT = 60 * 1024 * 1024
params = pltpu.CompilerParams(vmem_limit_bytes=VMEM_LIMIT)


def whole(count):
    return [pl.BlockSpec(memory_space=pltpu.VMEM)] * count


def shape(dims, dtype=BF16):
    return jax.ShapeDtypeStruct(dims, dtype)


def dot(left, right):
    return jnp.dot(left, right, preferred_element_type=F32)


def visible(place_col, place_row, seg_col, seg_row):
    return (seg_col[...] == seg_row[...]) & (place_row[...] <= place_col[...])


def attend_kernel(
    group_size,
    head_width,
    rows,
    gain,
    weights,
    cosine,
    sine,
    place_col,
    place_row,
    seg_col,
    seg_row,
    normed_out,
    queries_out,
    keys_out,
    values_out,
    logsum_out,
    context_out,
    mine_out,
    other_out,
):
    mix_width = (group_size + 2) * head_width
    values = rows[...].astype(F32)
    normed_out[...] = norm_forward(values, gain[...])[0].astype(BF16)
    mixed = dot(normed_out[...], weights[:, :mix_width])
    cos_table, sin_table = cosine[...], sine[...]
    scale = head_width ** (-0.5)
    width = group_size * head_width
    for head in range(group_size):
        part = slice(head * head_width, (head + 1) * head_width)
        queries_out[:, part] = (rotate(mixed[:, part], cos_table, sin_table) * scale).astype(BF16)
    keys_out[...] = rotate(mixed[:, width : width + head_width], cos_table, sin_table).astype(BF16)
    values_out[...] = mixed[:, width + head_width :].astype(BF16)
    allowed = visible(place_col, place_row, seg_col, seg_row)
    for head in range(group_size):
        part = slice(head * head_width, (head + 1) * head_width)
        scores = times_transposed(queries_out[:, part], keys_out[...])
        capped = jnp.where(allowed, soft_cap * jnp.tanh(scores / soft_cap), -jnp.inf)
        row_max = jnp.max(capped, axis=-1, keepdims=True)
        exp_scores = jnp.exp(capped - row_max)
        row_total = jnp.sum(exp_scores, axis=-1, keepdims=True)
        logsum_out[head] = row_max + jnp.log(row_total)
        context_out[:, part] = dot((exp_scores / row_total).astype(BF16), values_out[...]).astype(BF16)
    half = rows.shape[0] // 2
    other_out[...] = times_transposed(context_out[half:], weights[:, mix_width:]).astype(BF16)
    mine_out[...] = times_transposed(context_out[:half], weights[:, mix_width:])


def attend_back_kernel(
    group_size,
    head_width,
    slopes,
    weights,
    queries,
    keys,
    values,
    logsum,
    cosine,
    sine,
    place_col,
    place_row,
    seg_col,
    seg_row,
    mixed_out,
    mine_out,
    other_out,
):
    mix_width = (group_size + 2) * head_width
    width = group_size * head_width
    scale = head_width ** (-0.5)
    context_slope = dot(slopes[...], weights[:, mix_width:]).astype(BF16)
    cos_table, sin_table = cosine[...], -sine[...]
    allowed = visible(place_col, place_row, seg_col, seg_row)
    key_slope = jnp.zeros(keys.shape, F32)
    value_slope = jnp.zeros(values.shape, F32)
    for head in range(group_size):
        part = slice(head * head_width, (head + 1) * head_width)
        tanh_value = jnp.tanh(times_transposed(queries[:, part], keys[...]) / soft_cap)
        probs = jnp.where(allowed, jnp.exp(soft_cap * tanh_value - logsum[head]), 0.0)
        slope = context_slope[:, part]
        prob_slope = times_transposed(slope, values[...])
        value_slope += transposed(probs.astype(BF16), slope)
        inner_sum = jnp.sum(probs * prob_slope, axis=-1, keepdims=True)
        score_slope = (probs * (prob_slope - inner_sum) * (1.0 - tanh_value * tanh_value)).astype(BF16)
        query_slope = dot(score_slope, keys[...])
        key_slope += transposed(score_slope, queries[:, part])
        mixed_out[:, part] = rotate(query_slope * scale, cos_table, sin_table).astype(BF16)
    mixed_out[:, width : width + head_width] = rotate(key_slope, cos_table, sin_table).astype(BF16)
    mixed_out[:, width + head_width :] = value_slope.astype(BF16)
    half = slopes.shape[0] // 2
    other_out[...] = times_transposed(mixed_out[half:], weights[:, :mix_width]).astype(BF16)
    mine_out[...] = times_transposed(mixed_out[:half], weights[:, :mix_width])


root_two_pi = 0.7978845608028654
cubic = 0.044715


def gate_up_kernel(main, rows, weights, active_out, gate_out, up_out):
    result = dot(rows[...], weights[0])
    quarter = weights.shape[2] // 2
    bounds = [
        (slice(0, main), slice(main, 2 * main), slice(0, main)),
        (slice(2 * main, main + quarter), slice(main + quarter, 2 * quarter), slice(main, quarter)),
    ]
    for gate_part, up_part, part in bounds:
        gate, up = result[:, gate_part], result[:, up_part]
        square = gate * gate
        tanh_value = jnp.tanh(root_two_pi * gate * (1.0 + cubic * square))
        near = 0.5 * (1.0 + tanh_value)
        gelu = gate * near
        slope = near + 0.5 * gate * (1.0 - tanh_value * tanh_value) * root_two_pi * (
            1.0 + 3.0 * cubic * square
        )
        active_out[0, :, part] = (gelu * up).astype(BF16)
        gate_out[0, :, part] = (slope * up).astype(BF16)
        up_out[0, :, part] = gelu.astype(BF16)


def gate_up_call(rows, weights, main):
    count, width, columns = weights.shape
    height = rows.shape[0]
    quarter = columns // 2
    out_block = pl.BlockSpec((1, height, quarter), lambda i: (i, 0, 0))
    return pl.pallas_call(
        functools.partial(gate_up_kernel, main),
        grid=(count,),
        in_specs=[
            pl.BlockSpec((height, width), lambda i: (0, 0)),
            pl.BlockSpec((1, width, columns), lambda i: (i, 0, 0)),
        ],
        out_specs=[out_block] * 3,
        out_shape=[shape((count, height, quarter))] * 3,
        compiler_params=params,
    )(rows, weights)


def down_kernel(active, weights, *refs):
    out = refs[-1]
    total = times_transposed(active[0], weights[0])
    for place in range(1, active.shape[0]):
        total += times_transposed(active[place], weights[place])
    if len(refs) > 1:
        total += refs[0][...].astype(F32)
    out[...] = total.astype(out.dtype)


def down_call(active, weights, out_type, *received):
    count, height, quarter = active.shape
    width = weights.shape[1]
    tile = width // 3
    block = pl.BlockSpec((height, tile), lambda i: (0, i))
    return pl.pallas_call(
        down_kernel,
        grid=(3,),
        in_specs=[
            pl.BlockSpec((count, height, quarter), lambda i: (0, 0, 0)),
            pl.BlockSpec((count, tile, quarter), lambda i: (0, i, 0)),
        ]
        + [block] * len(received),
        out_specs=block,
        out_shape=shape((height, width), out_type),
        compiler_params=params,
    )(active, weights, *received)


def feed_back_kernel(main, *refs):
    slopes, (down, gate_up), factors = refs[:2], refs[2:4], refs[4:8]
    slope_outs, mine_out, other_out, total = refs[8:10], refs[10], refs[11], refs[12]
    step = pl.program_id(0)
    for place, sums in ((1, total), (0, mine_out)):
        active_slope = dot(slopes[place][...], down[0])
        gate_slope = (active_slope * factors[place][0].astype(F32)).astype(BF16)
        up_slope = (active_slope * factors[2 + place][0].astype(F32)).astype(BF16)
        slope_outs[place][0] = jnp.concatenate(
            [gate_slope[:, :main], up_slope[:, :main], gate_slope[:, main:], up_slope[:, main:]],
            axis=1,
        )
        product = times_transposed(slope_outs[place][0], gate_up[0])

        @pl.when(step == 0)
        def _():
            sums[...] = product

        @pl.when(step > 0)
        def _():
            sums[...] += product

    @pl.when(step == pl.num_programs(0) - 1)
    def _():
        other_out[...] = total[...].astype(BF16)


def feed_back_call(slopes, down, gate_up, gate_factors, up_factors, main):
    height, width = slopes[0].shape
    count, _, columns = gate_up.shape
    quarter = columns // 2
    whole_block = pl.BlockSpec((height, width), lambda i: (0, 0))
    once = pl.BlockSpec((height, width), lambda i: (0, 0), pipeline_mode=pl.Buffered(1))

    def each(rows, wide):
        return pl.BlockSpec((1, rows, wide), lambda i: (i, 0, 0))

    return pl.pallas_call(
        functools.partial(feed_back_kernel, main),
        grid=(count,),
        in_specs=[once] * 2
        + [each(width, quarter), each(width, columns)]
        + [each(height, quarter)] * 4,
        out_specs=[each(height, columns)] * 2 + [whole_block] * 2,
        out_shape=[shape((count, height, columns))] * 2
        + [shape((height, width), F32), shape((height, width))],
        scratch_shapes=[pltpu.VMEM((height, width), F32)],
        compiler_params=params,
    )(*slopes, down, gate_up, *gate_factors, *up_factors)


def weight_slope_kernel(left_mine, left_other, right_mine, right_other, out):
    total = transposed(left_mine[...], right_mine[0]) + transposed(left_other[...], right_other[0])
    out[0] = total.astype(BF16)


def weight_slope_call(lefts, rights):
    height, width = lefts[0].shape
    count, _, columns = rights[0].shape
    tile = width // 3
    left_block = pl.BlockSpec((height, tile), lambda i, j: (0, j))
    right_block = pl.BlockSpec((1, height, columns), lambda i, j: (i, 0, 0))
    return pl.pallas_call(
        weight_slope_kernel,
        grid=(count, 3),
        in_specs=[left_block] * 2 + [right_block] * 2,
        out_specs=pl.BlockSpec((1, tile, columns), lambda i, j: (i, j, 0)),
        out_shape=shape((count, width, columns)),
        compiler_params=params,
    )(*lefts, *rights)


def gate_up_adam_kernel(main, depth, *refs):
    pieces, (weight, mean, power), outs = refs[:DEPTH], refs[DEPTH : DEPTH + 3], refs[DEPTH + 3 :]
    rest = pieces[0].shape[1] // 2 - main
    quarters = []
    for place in range(DEPTH):
        step = (place - depth[0]) % DEPTH
        value = pieces[0][...]
        for ahead in range(1, DEPTH):
            value = jnp.where(step == ahead, pieces[ahead][...], value)
        quarters.append(value.astype(F32))
    for slot in range(2):
        begin = 2 * main + slot * rest
        gradient = jnp.concatenate(
            [value[:, slot * main : (slot + 1) * main] for value in quarters]
            + [value[:, begin : begin + rest] for value in quarters],
            axis=1,
        )
        result = adam_step(weight[:, slot], gradient, mean[:, slot], power[:, slot])
        for out, value in zip(outs, (gradient,) + result[:3]):
            out[:, slot] = value


def gate_up_adam_call(depth, pieces, weight, mean, power, main):
    block, columns = pieces[0].shape
    tile = 24 if block % 32 else 32
    piece_block = pl.BlockSpec((tile, columns), lambda i, depth: (i, 0))
    weight_block = pl.BlockSpec((tile,) + weight.shape[1:], lambda i, depth: (i, 0, 0))
    return pl.pallas_call(
        functools.partial(gate_up_adam_kernel, main),
        grid_spec=pltpu.PrefetchScalarGridSpec(
            num_scalar_prefetch=1,
            grid=(block // tile,),
            in_specs=[piece_block] * DEPTH + [weight_block] * 3,
            out_specs=[weight_block] * 4,
        ),
        out_shape=[shape(weight.shape, F32)] * 4,
        compiler_params=params,
    )(depth.reshape(1), *pieces, weight, mean, power)


def make_device(side_size):
    def per_device(
        inputs,
        segments,
        cotangent,
        project_weight,
        output_weight,
        gate_up_weight,
        down_weight,
        norm_gains,
        project_mean,
        project_power,
        output_mean,
        output_power,
        gate_up_mean,
        gate_up_power,
        down_mean,
        down_power,
        gains_mean,
        gains_power,
    ):
        depth, side, row, core = (lax.axis_index(name) for name in ("z", "x", "y", "c"))
        own_rows, width = inputs.shape
        block = project_weight.shape[0]
        head_width = project_weight.shape[3]
        slots = project_weight.shape[2]
        group_size = slots - 2
        kv_local = project_weight.shape[1]
        mix_width = kv_local * slots * head_width
        context_width = output_weight.shape[0]
        hidden = down_weight.shape[0]
        quarter = hidden // DEPTH
        main = quarter // 128 * 128
        total_rows = 4 * own_rows
        seq_count = total_rows // SEQ

        def arrange(value):
            lead = value.shape[0]
            value = value.reshape(lead, DEPTH, side_size, block).transpose(0, 2, 1, 3)
            return value.reshape(lead, width)

        def unarrange(value):
            lead = value.shape[0]
            value = value.reshape(lead, side_size, DEPTH, block).transpose(0, 2, 1, 3)
            return value.reshape(lead, width)

        attend_own = jnp.concatenate(
            [project_weight.astype(BF16).reshape(block, mix_width), output_weight.astype(BF16).T],
            axis=1,
        )
        rows_own = arrange(inputs)

        def gather_sequence(value):
            mine = jnp.concatenate([value, swap(value, "y")], axis=0)
            return jnp.concatenate([mine, swap(mine, "c")], axis=0)

        def scatter_sequence(mine, other, *earlier):
            mine = mine + swap(other, "c").astype(F32)
            if earlier:
                mine = after(mine, *earlier)
            return mine[:own_rows] + swap(mine[own_rows:].astype(BF16), "y").astype(F32)

        def gather_group(value):
            mine = jnp.concatenate(
                [value] + [from_ahead(value, "z", DEPTH, step) for step in range(1, DEPTH)], axis=0
            )
            return mine, swap(mine, "c")

        def scatter_group(mine):
            total = mine[:own_rows]
            for step in range(1, DEPTH):
                part = mine[step * own_rows : (step + 1) * own_rows].astype(BF16)
                total = total + from_ahead(part, "z", DEPTH, DEPTH - step).astype(F32)
            return total

        gains_parts = ordered(norm_gains, swap(norm_gains, "y"), row)
        gains_parts = ordered(gains_parts, swap(gains_parts, "c"), core)
        gains_parts = gains_parts.transpose(2, 1, 0, 3).reshape(1, 4 * block)
        gains_high = lax.optimization_barrier(gains_parts.astype(BF16))
        gains_low = (gains_parts - gains_high.astype(F32)).astype(BF16)
        attend_width = mix_width + context_width
        extra = 8
        attend_own = jnp.concatenate(
            [
                attend_own,
                jnp.pad(
                    jnp.concatenate([gains_high, gains_low], axis=0),
                    ((0, extra - 2), (0, attend_width - 4 * block)),
                ),
            ],
            axis=0,
        )

        def quartered(weight):
            whole = weight[:, : DEPTH * main].reshape(-1, DEPTH, main).transpose(1, 0, 2)
            rest = weight[:, DEPTH * main :].reshape(-1, DEPTH, quarter - main).transpose(1, 0, 2)
            return whole, rest

        def unquartered(whole, rest):
            return jnp.concatenate(
                [
                    whole.transpose(1, 0, 2).reshape(-1, DEPTH * main),
                    rest.transpose(1, 0, 2).reshape(-1, DEPTH * (quarter - main)),
                ],
                axis=1,
            )

        def over_z(pieces):
            return [from_ahead(piece, "z", DEPTH, step + 1) for step, piece in enumerate(pieces)]

        def quarter_pieces(pieces):
            return [
                lax.dynamic_index_in_dim(pieces, (depth - step) % DEPTH, 0, keepdims=False)
                for step in range(DEPTH)
            ]

        def by_depth(received):
            result = jnp.zeros((DEPTH * block, received[0].shape[1]), BF16)
            for step in range(DEPTH):
                result = lax.dynamic_update_slice(
                    result, received[step], ((depth + step) % DEPTH * block, 0)
                )
            return result

        def over_x(piece):
            return [from_ahead(piece, "x", side_size, ahead) for ahead in range(1, side_size)]

        gate_whole, gate_rest = quartered(gate_up_weight[:, 0].astype(BF16))
        up_whole, up_rest = quartered(gate_up_weight[:, 1].astype(BF16))
        gate_up_pieces = quarter_pieces(
            jnp.concatenate([gate_whole, up_whole, gate_rest, up_rest], axis=2)
        )
        down_pieces = quarter_pieces(jnp.concatenate(quartered(down_weight.astype(BF16).T), axis=2))

        attend_sent, rows_sent, *down_sent = gated([attend_own, rows_own, *down_pieces[1:]])
        down_received = over_z(down_sent)
        attend_across = [[attend_sent] + over_x(attend_sent)]
        rows_row = swap(rows_sent, "y")

        rows_half = jnp.concatenate([rows_own, rows_row], axis=0)
        rows_half, *attend_sent = gated(
            [rows_half, attend_own, attend_own, attend_own], *attend_across[0][1:], *down_received
        )
        rows_in = jnp.concatenate([rows_half, swap(rows_half, "c")], axis=0)
        down_own = by_depth(down_pieces[:1] + down_received)
        down_own = after(down_own, rows_row, *attend_across[0][1:])
        full_down = lax.all_gather(down_own, ("y", "x"), axis=0, tiled=True).reshape(2, width, quarter)
        near_pieces = [
            from_ahead(attend_sent[0], "z", DEPTH, 1),
            from_ahead(attend_sent[2], "z", DEPTH, 3),
        ]

        far_sent, *near_sent = gated([attend_sent[1], *near_pieces], rows_in)
        far_piece = from_ahead(far_sent, "z", DEPTH, 2)
        near_across = [[piece] + over_x(piece) for piece in near_sent]

        far_sent, *gate_up_sent = gated(
            [far_piece, *gate_up_pieces[1:]], *near_across[0][1:], *near_across[1][1:]
        )
        attend_across += [near_across[0], [far_sent] + over_x(far_sent), near_across[1]]
        gate_up_received = over_z(gate_up_sent)
        gate_up_own = by_depth(gate_up_pieces[:1] + gate_up_received)
        gate_up_own = after(gate_up_own, full_down, *attend_across[2][1:])
        full_gate_up = lax.all_gather(gate_up_own, ("y", "x"), axis=0, tiled=True)
        full_gate_up = full_gate_up.reshape(2, width, 2 * quarter)

        full_attend = jnp.zeros((side_size, DEPTH, block, attend_width), BF16)
        gains_all = jnp.zeros((side_size, DEPTH, 4, block), F32)
        for step in range(DEPTH):
            for ahead in range(side_size):
                piece = attend_across[step][ahead]
                place = ((side + ahead) % side_size, (depth + step) % DEPTH, 0, 0)
                full_attend = lax.dynamic_update_slice(full_attend, piece[None, None, :block], place)
                gains_pair = piece[block : block + 2, : 4 * block].astype(F32)
                gains_piece = (gains_pair[0] + gains_pair[1]).reshape(1, 1, 4, block)
                gains_all = lax.dynamic_update_slice(gains_all, gains_piece, place)
        full_attend = full_attend.reshape(width, attend_width)
        gains_all = gains_all.transpose(2, 0, 1, 3).reshape(4, width)

        residual_in = rows_own.astype(F32)
        factor_one = lax.rsqrt(jnp.mean(residual_in * residual_in, axis=-1, keepdims=True) + norm_eps)
        start = jnp.stack(
            [
                ((row ^ dr) * 2 + (core ^ dc)) * own_rows
                for dc in range(2)
                for dr in range(2)
            ]
        )
        order = (start[:, None] + jnp.arange(own_rows)[None, :]).reshape(total_rows)
        seg_parts = segments.reshape(2, 2, own_rows)
        seg_parts = rolled(rolled(seg_parts, row, 0), core, 1)
        seg_rows = seg_parts.transpose(1, 0, 2).reshape(total_rows)
        places = order
        half_width = head_width // 2
        frequency = rope_base ** (-2.0 * jnp.arange(half_width, dtype=F32) / head_width)
        angles = places.astype(F32)[:, None] * frequency[None, :]
        cosine_table, sine_table = jnp.cos(angles), jnp.sin(angles)
        tables = (
            cosine_table,
            sine_table,
            order[:, None],
            order[None, :],
            seg_rows[:, None],
            seg_rows[None, :],
        )
        rows_one, queries, key_vectors, value_rows, logsum, context_flat, mine, other = pl.pallas_call(
            functools.partial(attend_kernel, group_size, head_width),
            in_specs=whole(9),
            out_specs=whole(8),
            out_shape=[
                shape((total_rows, width)),
                shape((total_rows, context_width)),
                shape((total_rows, head_width)),
                shape((total_rows, head_width)),
                shape((group_size, total_rows, 1), F32),
                shape((total_rows, context_width)),
                shape((total_rows // 2, width), F32),
                shape((total_rows // 2, width)),
            ],
            compiler_params=params,
        )(rows_in, gains_all[:1], full_attend, *tables)
        attend_sum = scatter_sequence(mine, other)
        post_one, factor_two = norm_forward(attend_sum, gains_all[1])
        hidden_state = residual_in + post_one
        normed_two, factor_three = norm_forward(hidden_state, gains_all[2])

        rows_two = gather_group(after(normed_two.astype(BF16), *gate_up_received))
        activated, gate_factor, up_factor = zip(
            *[gate_up_call(rows, full_gate_up, main) for rows in rows_two]
        )
        received = swap(down_call(activated[1], full_down, BF16), "c")
        feed_sum = scatter_group(down_call(activated[0], full_down, F32, received))
        post_two, factor_four = norm_forward(feed_sum, gains_all[3])
        layer_output = unarrange((hidden_state + post_two).astype(BF16))

        upstream = arrange(cotangent).astype(F32)
        feed_slope, gain_four = norm_backward(feed_sum, factor_four, gains_all[3], upstream)
        feed_slope_rows = gather_group(feed_slope.astype(BF16))
        def ffn_total(left, right):
            return weight_slope_call(left, right).reshape(2 * width, -1)

        def reduce_ffn(total):
            return lax.psum_scatter(total, ("y", "x"), scatter_dimension=0, tiled=True)

        down_total = ffn_total(feed_slope_rows, activated)
        later_rows = gated(feed_slope_rows, down_total)
        slope_mine, slope_other, mine, other = feed_back_call(
            later_rows, full_down, full_gate_up, gate_factor, up_factor, main
        )
        received = swap(other, "c")
        normed_two_slope = scatter_group(mine + received.astype(F32))

        def owned(pieces):
            return rolled(jnp.stack(pieces), (DEPTH - depth) % DEPTH, 0)

        down_pieces = quarter_pieces(reduce_ffn(down_total).reshape(DEPTH, block, quarter))
        gate_up_total = ffn_total(rows_two, gated([slope_mine, slope_other], received))
        gate_up_mine = reduce_ffn(gate_up_total)

        hidden_part, gain_three = norm_backward(
            hidden_state, factor_three, gains_all[2], normed_two_slope
        )
        hidden_slope = upstream + hidden_part
        attend_slope, gain_two = norm_backward(attend_sum, factor_two, gains_all[1], hidden_slope)

        attend_slope = after(attend_slope, gate_up_total)

        slope_sent, *down_sent = gated([attend_slope.astype(BF16), *down_pieces[1:]])
        attend_slope_rows = gather_sequence(slope_sent)
        down_received = over_z(down_sent)
        down_parts = owned(down_pieces[:1] + down_received)
        down_grad = unquartered(down_parts[:, :, :main], down_parts[:, :, main:]).T.astype(F32)
        mixed_slope, mine, other = pl.pallas_call(
            functools.partial(attend_back_kernel, group_size, head_width),
            in_specs=whole(12),
            out_specs=whole(3),
            out_shape=[
                shape((total_rows, mix_width)),
                shape((total_rows // 2, width), F32),
                shape((total_rows // 2, width)),
            ],
            compiler_params=params,
        )(attend_slope_rows, full_attend, queries, key_vectors, value_rows, logsum, *tables)
        def gradient(left, right):
            total = transposed(left, right).astype(BF16)
            return total.reshape(side_size, DEPTH, block, right.shape[1])

        def side_parts(total):
            return [
                lax.dynamic_index_in_dim(total, (side + ahead) % side_size, 0, keepdims=False)
                for ahead in range(side_size)
            ]

        def over_side(parts):
            across = parts[0].astype(F32)
            for ahead in range(1, side_size):
                across = across + from_ahead(parts[ahead], "x", side_size, side_size - ahead).astype(F32)
            return across

        gate_up_pieces = quarter_pieces(gate_up_mine.reshape(DEPTH, block, 2 * quarter))
        project_parts = side_parts(gradient(rows_one, mixed_slope))
        sent = gated([*project_parts[1:], *gate_up_pieces[1:]], *down_received)
        gate_up_received = over_z(sent[side_size - 1 :])
        project_here = after(project_parts[0], *gate_up_received)
        project_across = over_side([project_here] + sent[: side_size - 1])
        normed_one_slope = scatter_sequence(mine, other)

        input_part, gain_one = norm_backward(residual_in, factor_one, gains_all[0], normed_one_slope)
        input_grad = unarrange(hidden_slope + input_part)

        gain_sum = jnp.stack([gain_one, gain_two, gain_three, gain_four], axis=0)
        lines = -(-4 * block // context_width)
        gain_sum = gain_sum.reshape(4, side_size, DEPTH, block).transpose(1, 2, 0, 3)
        gain_sum = gain_sum.reshape(side_size, DEPTH, 4 * block).astype(BF16)
        gain_sum = jnp.pad(gain_sum, ((0, 0), (0, 0), (0, lines * context_width - 4 * block)))
        gain_sum = jnp.pad(
            gain_sum.reshape(side_size, DEPTH, lines, context_width),
            ((0, 0), (0, 0), (0, extra - lines), (0, 0)),
        )
        context_later = after(context_flat, gate_up_received[0])
        output_total = jnp.concatenate(
            [gradient(attend_slope_rows, context_later), gain_sum], axis=2
        )

        output_parts = side_parts(output_total)
        project_pieces = quarter_pieces(project_across.astype(BF16))
        project_received = over_z(gated(project_pieces[1:], *gate_up_received))
        output_sent = gated(output_parts[1:], project_across)
        output_across = over_side(output_parts[:1] + output_sent)
        output_pieces = quarter_pieces(output_across.astype(BF16))
        output_received = over_z(gated(output_pieces[1:], *project_received))
        gate_up_sent = gated([gate_up_pieces[0], *gate_up_received], project_received[0])
        gate_up_grad, gate_up_new, gate_up_mean_new, gate_up_power_new = gate_up_adam_call(
            depth, gate_up_sent, gate_up_weight, gate_up_mean, gate_up_power, main
        )
        output_received = gated(output_received, gate_up_grad)

        def own_sum(across, received):
            mine = lax.dynamic_index_in_dim(across, depth, 0, keepdims=False)
            for part in received:
                mine = mine + part.astype(F32)
            return mine

        project_grad = own_sum(project_across, project_received).reshape(project_weight.shape)
        output_mine = own_sum(output_across, output_received)
        output_grad = output_mine[:block].T
        gain_part = output_mine[block : block + lines].reshape(1, -1)[:, : 4 * block]
        gain_part = gain_part.reshape(4, 2, 2, norm_gains.shape[1]).transpose(1, 2, 0, 3)
        for axis, place in (("y", row), ("c", core)):
            parts = rolled(gain_part, place, 0)
            gain_part = parts[0] + swap(parts[1], axis)
        gains_grad = gain_part

        project_new, project_mean_new, project_power_new, unused_one = adam_step(
            project_weight, project_grad, project_mean, project_power
        )
        output_new, output_mean_new, output_power_new, unused_two = adam_step(
            output_weight, output_grad, output_mean, output_power
        )
        down_grad = after(down_grad, project_received[0])
        down_new, down_mean_new, down_power_new, unused_four = adam_step(
            down_weight, down_grad, down_mean, down_power
        )
        unused_five, gains_mean_new, gains_power_new, gains_step = adam_step(
            norm_gains, gains_grad, gains_mean, gains_power
        )
        return (
            layer_output,
            input_grad,
            project_grad,
            project_new,
            project_mean_new,
            project_power_new,
            output_grad,
            output_new,
            output_mean_new,
            output_power_new,
            gate_up_grad,
            gate_up_new,
            gate_up_mean_new,
            gate_up_power_new,
            down_grad,
            down_new,
            down_mean_new,
            down_power_new,
            gains_grad,
            gains_step,
            gains_mean_new,
            gains_power_new,
        )

    return per_device


def solution(mesh):
    side_size = mesh.shape["fsdp"] // DEPTH
    fine = Mesh(mesh.devices.reshape(DEPTH, side_size, 2, 2), ("z", "x", "y", "c"))
    fsdp = ("z", "x")
    tp = ("y", "c")
    both = fsdp + tp
    rows = P(both, None)
    project = P(fsdp, tp, None, None)
    across = P(tp, fsdp)
    gate_up = P(fsdp, None, tp)
    gains = P(None, both)
    in_specs = (
        (rows, P(fsdp), rows, project, across, gate_up, across, gains)
        + (project,) * 2
        + (across,) * 2
        + (gate_up,) * 2
        + (across,) * 2
        + (gains,) * 2
    )
    out_specs = (
        (rows, rows)
        + (project,) * 4
        + (across,) * 4
        + (gate_up,) * 4
        + (across,) * 4
        + (gains,) * 4
    )
    return jax.shard_map(
        make_device(side_size), mesh=fine, in_specs=in_specs, out_specs=out_specs, check_vma=False
    )
```
